128 devices in a mesh: lat: 8 (over y, x_lo), lon: 16 (over x_hi, z, core).
Axes of the slice: x: 4 (x_hi: 2, x_lo: 2; x = x_hi * 2 + x_lo), y: 4, z: 4, core: 2. Of those that a mesh axis runs over, the one named last changes fastest.
Arguments:
- innovation: float32 [32, 524288], P(None, ('lat', 'lon')), may hold values from -6 to 6
- jacobian: float32 [32, 4, 524288], P(None, None, ('lat', 'lon')), may hold values from -1 to 1
- channel_count: int32 [524288], P(('lat', 'lon')), may hold values from 1 to 32
- owner: int32 [524288, 1], P(('lat', 'lon')), may hold values from 0 to 127; in each aligned block of 4096 rows (0 to 4095, 4096 to 8191, ...) at most 128 rows name the same one
- footprint: int32 [8, 524288], P(None, ('lat', 'lon')), may hold values from 0 to 8191
- weight: float32 [8, 524288], P(None, ('lat', 'lon')), may hold values from 0.3 to 1
- perturbation: float32 [40, 4, 256, 4096], P(None, None, 'lat', 'lon'), may hold values from -6 to 6
- scale_first: float32 [256, 4096], P('lat', 'lon'), may hold values from 0.12 to 0.245
- scale_second: float32 [256, 4096], P('lat', 'lon'), may hold values from 0.12 to 0.245
Outputs:
- gradient: float32 [40, 4, 256, 4096], P(None, None, 'lat', 'lon')
The draws below stay inside these ranges and needn't reach their ends.
Inputs may be any that keep to these rules, and one draw needn't show every extreme that they name: Among the 4096 observations of one device, no owner is named more than 128 times, a bound that some block reaches.
All inputs are finite; a program needn't handle non-finite values.
Results may differ from the reference program's by a relative error of at most 0.00011.
Values sent between devices are 32-bit elements; how exact they have to be, the bound alone decides.
A program may use at most 128 MiB of HBM per device.

```python
import math
import jax
import jax.numpy as jnp
import numpy as np
from jax import lax

MEMBERS = 40
LEV = 4
CH = 32
FP = 8
STEPS = 3
CLAT = 32
CLON = 256
OBS_DEV = 4096
CAP = 128
NLAT = 256
NLON = 4096
NOBS = 524288
DEVICES = 128


def set_ends(result, rng, low, high):
    longest = result.shape.index(max(result.shape))
    spots = []
    for shift in (0, 1):
        where = [jax.random.randint(jax.random.fold_in(rng, axis), (), 0, length) for axis, length in enumerate(result.shape)]
        where[longest] = (where[longest] + shift) % result.shape[longest]
        spots.append(tuple(where))
    return result.at[spots[0]].set(low).at[spots[1]].set(high)


def block_levels(rng, dims, split, smallest, high):
    gain, own = 1.0, jax.random.fold_in(rng, 6)
    for dim, parts in split:
        heights = jnp.exp(jax.random.uniform(jax.random.fold_in(own, dim), (parts,), jnp.float32, smallest / len(split), high / len(split)))
        gain = gain * jnp.repeat(heights, dims[dim] // parts).reshape([-1 if axis == dim else 1 for axis in range(len(dims))])
    return gain


def routed_block(rng, own, number, rows, count, top, reach, slope):
    sequence = jax.random.permutation(rng, count)
    heavy_load, common = shares(count, rows * top, reach, slope, True), shares(count, rows * top, reach, slope, False)
    places = jnp.arange(count)

    def named(sizes, rotation):
        used = int((sizes > 0).sum())
        fixed = max(1, used // 4)
        moved = fixed + (places - fixed + rotation * (used - fixed)) % max(1, count - fixed)
        return jnp.zeros((count,), jnp.int32).at[sequence[jnp.where(places < fixed, places, moved)]].set(jnp.asarray(sizes, jnp.int32))

    sizes = jnp.where(number % 4 == 0, named(heavy_load, number // 4), named(common, number - number // 4 - 1))
    mixed = jax.random.permutation(jax.random.fold_in(own, 3), count)
    giver, sink = mixed[0:count // 2 * 2:2], mixed[1:count // 2 * 2:2]
    room = jnp.minimum(sizes[giver] - 1, reach - sizes[sink]) // 2
    room = jnp.where((giver == sequence[0]) | (sink == sequence[0]) | (sizes[sink] == 0), 0, jnp.maximum(room, 0))
    moved = jax.random.randint(jax.random.fold_in(own, 4), (count // 2,), 0, 1 << 20) % (room + 1)
    sizes = sizes.at[giver].add(-moved).at[sink].add(moved)
    items = jnp.searchsorted(jnp.cumsum(sizes), jnp.arange(rows * top), side="right").astype(jnp.int32)
    grid = items.reshape(top, rows).T
    grid = grid[jax.random.permutation(jax.random.fold_in(own, 1), rows)]
    rotation = jax.random.randint(jax.random.fold_in(own, 2), (rows, 1), 0, top)
    return jnp.take_along_axis(grid, (jnp.arange(top)[None, :] + rotation) % top, axis=1)


def shares(amount, total, limit, lean, full):
    loads = [(1 << 20) // math.isqrt(standing ** lean) + 1 for standing in range(1, amount + 1)]
    largest = limit if full else min(limit, max(-(-total // amount), total * loads[0] // sum(loads)))
    least = 1 if total - largest >= amount - 1 else 0
    counts, spare = [largest] + [least] * (amount - 1), total - largest - least * (amount - 1)
    while spare > 0:
        movable = [i for i in range(1, amount) if counts[i] < largest] or [i for i in range(1, amount) if counts[i] < limit]
        pool, left = sum([loads[i] for i in movable]), spare
        for i in movable:
            addition = min(limit - counts[i], max(1, left * loads[i] // pool), spare)
            counts[i] = counts[i] + addition
            spare = spare - addition
    return np.array(counts)


def scatter_about(own_key, shape, width, bound, shards=(), held_as=jnp.bfloat16):
    level = block_levels(own_key, shape, shards, -0.22, 0.18) if shards else 1.0
    entries = jax.random.normal(own_key, shape, jnp.float32) * width * level
    return jnp.minimum(jnp.maximum(entries, -bound), bound).astype(held_as)


def setup_inputs(seed: int = 0) -> dict:
    seeds = jax.random.split(jax.random.key(seed), 10)
    innovation = scatter_about(seeds[0], (CH, NOBS), 1.0, 6.0, ((1, 128),), jnp.float32)
    jacobian = scatter_about(seeds[1], (CH, LEV, NOBS), CH ** -0.5, 1.0, ((2, 128),), jnp.float32)
    channel_count = set_ends(jax.random.randint(seeds[2], (NOBS,), 1, CH + 1), jax.random.fold_in(seeds[2], 1), 1, CH).astype(jnp.int32)
    owner_keys = jax.random.split(jax.random.fold_in(seeds[3], 1), NOBS // OBS_DEV)
    owner_turns = jax.random.permutation(jax.random.fold_in(seeds[3], 3), NOBS // OBS_DEV)
    owner = jax.vmap(lambda own, number: routed_block(jax.random.fold_in(seeds[3], 2), own, number, OBS_DEV, DEVICES, 1, CAP, 2))(owner_keys, owner_turns).reshape((NOBS, 1))
    footprint = set_ends(jax.random.randint(seeds[4], (FP, NOBS), 0, CLAT * CLON), jax.random.fold_in(seeds[4], 1), 0, (CLAT * CLON) - 1).astype(jnp.int32)
    weight = jnp.clip(jnp.exp(math.log(1.0) - 1.2039728 * jax.random.uniform(seeds[5], (FP, NOBS), jnp.float32) ** block_levels(seeds[5], (FP, NOBS), ((1, 128),), -0.2, 0.2)), 0.3, 1.0)
    perturbation = scatter_about(seeds[6], (MEMBERS, LEV, NLAT, NLON), 1.0, 6.0, ((2, 8), (3, 16)), jnp.float32)
    scale_first = jnp.clip(jnp.exp(math.log(0.245) - 0.7137665 * jax.random.uniform(seeds[7], (NLAT, NLON), jnp.float32) ** block_levels(seeds[7], (NLAT, NLON), ((0, 8), (1, 16)), -0.2, 0.2)), 0.12, 0.245)
    scale_second = jnp.clip(jnp.exp(math.log(0.245) - 0.7137665 * jax.random.uniform(seeds[8], (NLAT, NLON), jnp.float32) ** block_levels(seeds[8], (NLAT, NLON), ((0, 8), (1, 16)), -0.2, 0.2)), 0.12, 0.245)
    return dict(innovation=innovation, jacobian=jacobian, channel_count=channel_count, owner=owner, footprint=footprint, weight=weight, perturbation=perturbation, scale_first=scale_first, scale_second=scale_second)


def diffuse(field, kappa):
    padded = jnp.pad(field, ((0, 0), (1, 1), (0, 0)))
    north = padded[:, :-2, :]
    south = padded[:, 2:, :]
    west = jnp.roll(field, 1, axis=2)
    east = jnp.roll(field, -1, axis=2)
    return field + kappa * (north + south + west + east - 4.0 * field)


def reference(innovation, jacobian, channel_count, owner, footprint, weight, perturbation, scale_first, scale_second):
    tiles_lon = NLON // CLON
    chan_index = jnp.arange(CH, dtype=jnp.int32)[:, None]
    live = (chan_index < channel_count[None, :]).astype(jnp.float32)
    profile = jnp.sum(jacobian * (innovation * live)[:, None, :], axis=0)
    target = owner[:, 0]
    tile_row = target // tiles_lon
    tile_col = target % tiles_lon
    grid_row = tile_row[None, :] * CLAT + footprint // CLON
    grid_col = tile_col[None, :] * CLON + footprint % CLON
    flat_cell = (grid_row * NLON + grid_col).reshape(-1).astype(jnp.int32)
    contrib = (weight[None, :, :] * profile[:, None, :]).reshape(LEV, -1)
    adjoint = jnp.zeros((LEV, NLAT * NLON), jnp.float32).at[:, flat_cell].add(contrib)
    adjoint = adjoint.reshape(LEV, NLAT, NLON)

    def member(pert):
        field = pert * adjoint
        for step_a in range(STEPS):
            field = diffuse(field, scale_first)
        for step_b in range(STEPS):
            field = diffuse(field, scale_second)
        return field

    return lax.map(member, perturbation)
```

```python
import jax
import jax.numpy as jnp
from jax import lax
from jax.experimental import pallas as pl
from jax.experimental.pallas import tpu as pltpu
from jax.sharding import PartitionSpec as P

STEPS = 3
HALO = 2 * STEPS
LANES = 128
SUB = 8
MESH = pl.DeviceIdType.MESH
F32 = jnp.float32
BF16 = jnp.bfloat16
I32 = jnp.int32
NT = (((1,), (1,)), ((), ()))


def iota(shape, dim):
    return lax.broadcasted_iota(I32, shape, dim)


def dot(a, b):
    return jnp.dot(a, b, preferred_element_type=F32)


def dot_nt(a, b):
    return lax.dot_general(a, b, NT, preferred_element_type=F32)


def vmem(limit, **kw):
    return pltpu.CompilerParams(vmem_limit_bytes=limit << 20, **kw)


def row_at(r, ct):
    return (r // SUB) * 16 + ct * SUB + r % SUB


def edges_kernel(p_ref, n_ref, s_ref, w_ref, e_ref):
    group = iota((SUB, LANES), 1) // SUB

    def load(r, ct):
        return p_ref[pl.ds(row_at(r, ct), SUB, stride=64), :]

    for r in range(HALO):
        for ct in range(2):
            n_ref[0, r, ct] = load(r, ct)
            s_ref[0, r, ct] = load(32 - HALO + r, ct)
    for b in range(2):
        w = jnp.zeros((SUB, LANES), F32)
        e = jnp.zeros((SUB, LANES), F32)
        for j in range(16):
            w = jnp.where(group == j, pltpu.roll(load(16 * b + j, 0), 8 * j, 1), w)
            e = jnp.where(group == j, pltpu.roll(load(16 * b + j, 1), (8 * j + 8) % LANES, 1), e)
        w_ref[0, b] = w
        e_ref[0, b] = e


def edges(view, groups):
    rows = jax.ShapeDtypeStruct((groups, HALO, 2, SUB, LANES), F32)
    cols = jax.ShapeDtypeStruct((groups, 2, SUB, LANES), F32)
    row_spec = pl.BlockSpec((1, HALO, 2, SUB, LANES), lambda g: (g, 0, 0, 0, 0))
    col_spec = pl.BlockSpec((1, 2, SUB, LANES), lambda g: (g, 0, 0, 0))
    return pl.pallas_call(
        edges_kernel,
        grid=(groups,),
        out_shape=(rows, rows, cols, cols),
        in_specs=[pl.BlockSpec((512, LANES), lambda g: (g, 0))],
        out_specs=(row_spec, row_spec, col_spec, col_spec),
        compiler_params=vmem(32),
        name="edges",
    )(view)


def pack_kernel(inn_ref, jac_ref, cc_ref, own_ref, foot_ref, wgt_ref, out_ref,
                tot_ref, acc_ref, sorted_ref, cnt_v, cnt_s, sem):
    chans, obs = inn_ref.shape
    blk = 256
    ones = jnp.ones((2 * blk, LANES), BF16)
    ones8 = jnp.ones((SUB, 2 * blk), BF16)
    tot_ref[...] = jnp.zeros_like(tot_ref)

    def count(i, row):
        own = own_ref[:, pl.ds(pl.multiple_of(i * 2 * blk, 2 * blk), 2 * blk)]
        hot = (iota((LANES, 2 * blk), 0) == own).astype(F32).astype(BF16)
        tot_ref[...] += dot(hot, ones)
        return row + dot_nt(ones8, hot)

    tot_row = lax.fori_loop(0, obs // (2 * blk), count, jnp.zeros((SUB, LANES), F32))
    upper = (iota((LANES, LANES), 0) < iota((LANES, LANES), 1)).astype(F32).astype(BF16)
    lower = (iota((LANES, LANES), 0) > iota((LANES, LANES), 1)).astype(F32).astype(BF16)
    cnt_v[0:SUB] = dot(tot_row.astype(BF16), upper).astype(I32)
    cnt_v[SUB:2 * SUB] = tot_row.astype(I32)
    to_smem = pltpu.make_async_copy(cnt_v, cnt_s, sem)
    to_smem.start()
    tot_ref[...] = dot(lower, tot_ref[...].astype(BF16))
    upper_b = (iota((blk, blk), 0) < iota((blk, blk), 1)).astype(F32).astype(BF16)
    acc_ref[...] = jnp.zeros_like(acc_ref)

    def block(i, carry):
        at = pl.ds(pl.multiple_of(i * blk, blk), blk)
        own = own_ref[:, at]
        hot = iota((LANES, blk), 0) == own
        hot_b = hot.astype(F32).astype(BF16)
        base = tot_ref[...]
        place = dot(hot_b, upper_b) + jnp.concatenate([base, base], axis=1)
        tot_ref[...] = base + dot(hot_b, ones[:blk])
        pos = jnp.sum(jnp.where(hot, place, 0.0), axis=0, keepdims=True).astype(I32)
        cc = cc_ref[:, at]
        prof = jnp.zeros((4, blk), F32)
        for c in range(chans):
            live = jnp.where(cc > c, inn_ref[c:c + 1, at], 0.0)
            prof = prof + jac_ref[c, :, at] * live
        full = jnp.concatenate([wgt_ref[:, at], foot_ref[:, at].astype(F32), prof, prof], axis=0)
        head = full.astype(BF16).astype(F32)
        both = jnp.concatenate([head, full - head], axis=0)
        hi = lax.shift_right_logical(pos, 8)
        lo = lax.bitwise_and(pos, 255)
        spread = jnp.concatenate([jnp.where(hi == h, both, 0.0) for h in range(obs // blk)], axis=0)
        hot_lo = (iota((blk, blk), 0) == lo).astype(F32).astype(BF16)
        acc_ref[...] += dot_nt(spread.astype(BF16), hot_lo)
        return carry

    lax.fori_loop(0, obs // blk, block, 0)
    for h in range(obs // blk):
        s = acc_ref[48 * h:48 * h + 24, :] + acc_ref[48 * h + 24:48 * h + 48, :]
        sorted_ref[2 * h] = s[:, :LANES]
        sorted_ref[2 * h + 1] = s[:, LANES:]
    for t in range(2):
        sorted_ref[obs // LANES + t] = jnp.zeros((24, LANES), F32)
    to_smem.wait()
    lane = iota((24, LANES), 1)

    def window(i, carry):
        for u in range(4):
            d = i * 4 + u
            first = cnt_s[0, d]
            number = cnt_s[SUB, d]
            t = lax.shift_right_logical(first, 7)
            off = lax.bitwise_and(first, 127)
            y = jnp.where(lane >= off, sorted_ref[t], sorted_ref[t + 1])
            y = pltpu.roll(y, lax.bitwise_and(LANES - off, 127), 1)
            out_ref[pl.ds(pl.multiple_of(d * 24, 8), 24), :] = jnp.where(lane < number, y, 0.0)
        return carry

    lax.fori_loop(0, LANES // 4, window, 0)


def pack(inn, jac, cc, own, foot, wgt):
    obs = inn.shape[1]
    return pl.pallas_call(
        pack_kernel,
        out_shape=jax.ShapeDtypeStruct((24 * LANES, LANES), F32),
        in_specs=[pl.BlockSpec(memory_space=pltpu.VMEM)] * 6,
        out_specs=pl.BlockSpec(memory_space=pltpu.VMEM),
        scratch_shapes=[
            pltpu.VMEM((LANES, LANES), F32),
            pltpu.VMEM((48 * (obs // 256), 256), F32),
            pltpu.VMEM((obs // LANES + 2, 24, LANES), F32),
            pltpu.VMEM((2 * SUB, LANES), I32),
            pltpu.SMEM((2 * SUB, LANES), I32),
            pltpu.SemaphoreType.DMA,
        ],
        compiler_params=vmem(40),
        name="pack",
    )(inn, jac, cc, own, foot, wgt)


DIRS = ((1, 0), (-1, 0), (0, 1), (0, -1), (1, 1), (1, -1), (-1, 1), (-1, -1))


def halo_copies(src, mid, wb, eb, send, recv, n_lat, n_lon):
    rows = src.shape[0]
    lat, lon = lax.axis_index("lat"), lax.axis_index("lon")
    copies = []
    for k, (dy, dx) in enumerate(DIRS):
        take = {1: pl.ds(rows - HALO, HALO), -1: pl.ds(0, HALO), 0: pl.ds(0, rows)}[dy]
        put = {1: pl.ds(0, HALO), -1: pl.ds(HALO + rows, HALO), 0: pl.ds(HALO, rows)}[dy]
        if dx == 0:
            s, d = src.at[take], mid.at[put]
        elif dx == 1:
            s, d = src.at[take, :, pl.ds(LANES, LANES)], wb.at[put]
        else:
            s, d = src.at[take, :, pl.ds(0, LANES)], eb.at[put]
        to = (lat + dy, lax.rem(lon + dx + n_lon, n_lon))
        copies.append(pltpu.make_async_remote_copy(
            src_ref=s, dst_ref=d, send_sem=send.at[k], recv_sem=recv.at[k],
            device_id=to, device_id_type=MESH))
    return copies


def when_lat(dy, lat, n_lat, fn):
    if dy == 0:
        fn()
    elif dy == 1:
        pl.when(lat < n_lat - 1)(fn)
    else:
        pl.when(lat > 0)(fn)


def halo_start(copies, lat, n_lat):
    for k, (dy, dx) in enumerate(DIRS):
        when_lat(dy, lat, n_lat, copies[k].start)


def halo_wait(copies, lat, n_lat):
    for k, (dy, dx) in enumerate(DIRS):
        when_lat(dy, lat, n_lat, copies[k].wait_send)
        when_lat(-dy, lat, n_lat, copies[k].wait_recv)


def halo_clear(mid, wb, eb, rows):
    for ref in (mid, wb, eb):
        for r in list(range(HALO)) + list(range(HALO + rows, 2 * HALO + rows)):
            ref[r] = jnp.zeros(ref.shape[1:], F32)


def halo_row(R, src, mid, wb, eb, rows):
    inner = src[R - HALO] if HALO <= R < HALO + rows else mid[R]
    lane = iota((4, LANES), 1)
    side = jnp.where(lane < HALO, eb[R], wb[R])
    return jnp.concatenate([inner, side], axis=1)


def route_kernel(n_lat, n_lon, s_ref, kap_ref, o_ref, kk_ref, mid, wb, eb,
                 send_sem, recv_sem, own_sem, hs, hr):
    lat, lon = lax.axis_index("lat"), lax.axis_index("lon")
    n = n_lat * n_lon
    me = lat * n_lon + lon
    rows = kap_ref.shape[0]
    halo_clear(mid, wb, eb, rows)
    bar = pltpu.get_barrier_semaphore()

    def place(k):
        t = lax.rem(me + k, n)
        return t, (lax.div(t, n_lon), lax.rem(t, n_lon))

    def signal(k, c):
        pl.semaphore_signal(bar, inc=1, device_id=place(k)[1], device_id_type=MESH)
        return c

    lax.fori_loop(1, n, signal, 0)
    own = pltpu.make_async_copy(s_ref.at[me, pl.ds(0, 5)], o_ref.at[me, pl.ds(0, 5)], own_sem)
    own.start()
    pl.semaphore_wait(bar, n - 1)
    copies = halo_copies(kap_ref, mid, wb, eb, hs, hr, n_lat, n_lon)
    halo_start(copies, lat, n_lat)

    def send(k, c):
        t, to = place(k)
        pltpu.make_async_remote_copy(
            src_ref=s_ref.at[t, pl.ds(0, 5)], dst_ref=o_ref.at[me, pl.ds(0, 5)],
            send_sem=send_sem, recv_sem=recv_sem, device_id=to, device_id_type=MESH).start()
        return c

    lax.fori_loop(1, n, send, 0)
    halo_wait(copies, lat, n_lat)
    for R in range(rows + 2 * HALO):
        x = halo_row(R, kap_ref, mid, wb, eb, rows)
        for q in range(4):
            kk_ref[q, R] = jnp.broadcast_to(x[q:q + 1], (SUB, x.shape[1]))
    own.wait()
    rest = pltpu.make_async_remote_copy(
        src_ref=s_ref.at[pl.ds(0, n - 1), pl.ds(0, 5)], dst_ref=o_ref.at[pl.ds(0, n - 1), pl.ds(0, 5)],
        send_sem=send_sem, recv_sem=recv_sem, device_id=place(1)[1], device_id_type=MESH)
    rest.wait_send()
    rest.wait_recv()


def halo_scratch(rows):
    return [
        pltpu.VMEM((rows + 2 * HALO, 4, 2 * LANES), F32),
        pltpu.VMEM((rows + 2 * HALO, 4, LANES), F32),
        pltpu.VMEM((rows + 2 * HALO, 4, LANES), F32),
    ]


def route(windows, kap, n_lat, n_lon):
    rows = kap.shape[0]
    any_spec = pl.BlockSpec(memory_space=pltpu.VMEM)
    return pl.pallas_call(
        lambda *refs: route_kernel(n_lat, n_lon, *refs),
        out_shape=(jax.ShapeDtypeStruct(windows.shape, F32),
                   jax.ShapeDtypeStruct((4, rows + 2 * HALO, SUB, 3 * LANES), F32)),
        in_specs=[any_spec, any_spec],
        out_specs=(any_spec, any_spec),
        scratch_shapes=halo_scratch(rows) + [
            pltpu.SemaphoreType.DMA, pltpu.SemaphoreType.DMA, pltpu.SemaphoreType.DMA,
            pltpu.SemaphoreType.DMA((8,)), pltpu.SemaphoreType.DMA((8,)),
        ],
        compiler_params=vmem(40, collective_id=0, has_side_effects=True),
        name="route",
    )(windows, kap)


def total_kernel(rx_ref, out_ref, buf, acc, cnt_v, cnt_s, sem):
    n = rx_ref.shape[0] // 24
    mask = jnp.concatenate(
        [rx_ref[pl.ds(24 * SUB * i, SUB, stride=24), :] for i in range(n // SUB)], axis=0)
    mask = jnp.where(mask > 0.0, 1.0, 0.0).astype(BF16)
    row = dot_nt(jnp.ones((SUB, LANES), BF16), mask)
    upper = (iota((LANES, LANES), 0) < iota((LANES, LANES), 1)).astype(F32).astype(BF16)
    cnt_v[0:SUB] = dot(row.astype(BF16), upper).astype(I32)
    cnt_v[SUB:2 * SUB] = row.astype(I32)
    to_smem = pltpu.make_async_copy(cnt_v, cnt_s, sem)
    to_smem.start()
    acc[...] = jnp.zeros_like(acc)
    to_smem.wait()
    lane = iota((24, LANES), 1)

    def append(i, cur):
        for u in range(4):
            s = i * 4 + u
            first = cnt_s[0, s]
            number = cnt_s[SUB, s]
            t = lax.shift_right_logical(first, 7)
            off = lax.bitwise_and(first, 127)
            y = pltpu.roll(rx_ref[pl.ds(pl.multiple_of(s * 24, 8), 24), :], off, 1)
            y = jnp.where(iota((24, LANES), 0) < 20, y, 0.0)
            merged = jnp.where(lane >= off, y, cur)
            buf[t] = merged
            cur = jnp.where(off + number >= LANES, jnp.where(lane < off, y, 0.0), merged)
        return cur

    cur = lax.fori_loop(0, n // 4, append, jnp.zeros((24, LANES), F32))
    points = cnt_s[0, n - 1] + cnt_s[SUB, n - 1]
    buf[lax.shift_right_logical(points, 7)] = cur
    sub = iota((SUB, LANES), 0)
    col_ids = iota((2 * LANES, LANES), 0)

    def tile(i, carry):
        w = buf[i, 0:8]
        cell = buf[i, 8:16].astype(I32)
        half = buf[i, 16:24]
        prof = half + pltpu.roll(half, 4, 0)
        cell_row = lax.shift_right_logical(cell, 8)
        cell_col = lax.bitwise_and(cell, 255)
        left, right = [], []
        for f in range(SUB):
            v = w[f:f + 1] * prof
            head = v.astype(BF16).astype(F32)
            both = jnp.where(sub < 4, head, v - head)
            r = jnp.broadcast_to(cell_row[f:f + 1], (SUB, LANES))
            left.append(jnp.concatenate(
                [jnp.where(r == k, both, 0.0) for k in range(32)], axis=0).astype(BF16))
            right.append(jnp.where(col_ids == cell_col[f:f + 1], 1.0, 0.0).astype(BF16))
        acc[...] += dot_nt(jnp.concatenate(left, axis=1), jnp.concatenate(right, axis=1))
        return carry

    lax.fori_loop(0, lax.shift_right_logical(points + 127, 7), tile, 0)
    for r in range(32):
        x = acc[SUB * r:SUB * r + SUB, :]
        out_ref[r] = (x + pltpu.roll(x, 4, 0))[0:4]


def total(rx, rows, cols):
    n = rx.shape[0] // 24
    return pl.pallas_call(
        total_kernel,
        out_shape=jax.ShapeDtypeStruct((rows, 4, cols), F32),
        in_specs=[pl.BlockSpec(memory_space=pltpu.VMEM)],
        out_specs=pl.BlockSpec(memory_space=pltpu.VMEM),
        scratch_shapes=[
            pltpu.VMEM((n + 1, 24, LANES), F32),
            pltpu.VMEM((SUB * rows, cols), F32),
            pltpu.VMEM((2 * SUB, LANES), I32),
            pltpu.SMEM((2 * SUB, LANES), I32),
            pltpu.SemaphoreType.DMA,
        ],
        compiler_params=vmem(40),
        name="total",
    )(rx)


def widen_kernel(n_lat, n_lon, a_ref, out_ref, mid, wb, eb, hs, hr):
    lat, lon = lax.axis_index("lat"), lax.axis_index("lon")
    rows = a_ref.shape[0]
    halo_clear(mid, wb, eb, rows)
    bar = pltpu.get_barrier_semaphore()
    for dy, dx in DIRS:
        def signal(dy=dy, dx=dx):
            pl.semaphore_signal(
                bar, inc=1, device_id=(lat + dy, lax.rem(lon + dx + n_lon, n_lon)),
                device_id_type=MESH)
        when_lat(dy, lat, n_lat, signal)
    pl.semaphore_wait(bar, 2 + 3 * jnp.minimum(lat, 1) + 3 * jnp.minimum(n_lat - 1 - lat, 1))
    copies = halo_copies(a_ref, mid, wb, eb, hs, hr, n_lat, n_lon)
    halo_start(copies, lat, n_lat)
    halo_wait(copies, lat, n_lat)
    for R in range(rows + 2 * HALO):
        x = halo_row(R, a_ref, mid, wb, eb, rows)
        out_ref[R] = jnp.concatenate([x, x], axis=0)


def widen(adjoint, n_lat, n_lon):
    rows = adjoint.shape[0]
    spec = pl.BlockSpec(memory_space=pltpu.VMEM)
    return pl.pallas_call(
        lambda *refs: widen_kernel(n_lat, n_lon, *refs),
        out_shape=jax.ShapeDtypeStruct((rows + 2 * HALO, SUB, 3 * LANES), F32),
        in_specs=[spec],
        out_specs=spec,
        scratch_shapes=halo_scratch(rows) + [
            pltpu.SemaphoreType.DMA((8,)), pltpu.SemaphoreType.DMA((8,))],
        compiler_params=vmem(40, collective_id=1, has_side_effects=True),
        name="widen",
    )(adjoint)


def diffuse_kernel(p_ref, nh_ref, sh_ref, pw_ref, pe_ref, cn_ref, cs_ref, adj_ref, kk_ref,
                   out_ref, x_ref):
    rows = 32
    ext = rows + 2 * HALO
    lane = iota((SUB, LANES), 1)

    def side(w, w_at, e, e_at):
        w = pltpu.roll(w, (LANES - 8 - w_at) % LANES, 1)
        e = pltpu.roll(e, (LANES - e_at) % LANES, 1)
        return jnp.where(lane < 8, e, w)

    for R in range(ext):
        r = R - HALO
        if r < 0:
            mid = [nh_ref[0, R, ct] for ct in range(2)]
            s = side(cn_ref[0], 80 + 8 * R, cn_ref[0], 16 + 8 * R)
        elif r >= rows:
            mid = [sh_ref[0, r - rows, ct] for ct in range(2)]
            s = side(cs_ref[0], 8 * (r - rows), cs_ref[0], 64 + 8 * (r - rows))
        else:
            mid = [p_ref[pl.ds(row_at(r, ct), SUB, stride=64), :] for ct in range(2)]
            s = side(pw_ref[0, r // 16], 8 * (r % 16), pe_ref[0, r // 16], 8 * (r % 16))
        x_ref[R] = jnp.concatenate(mid + [s], axis=1) * adj_ref[R]
    for step in range(1, 2 * STEPS + 1):
        q = 0 if step <= STEPS else 2
        north, center = x_ref[step - 1], x_ref[step]
        for R in range(step, ext - step):
            south = x_ref[R + 1]
            west = pltpu.roll(center, 1, 1)
            east = pltpu.roll(center, 3 * LANES - 1, 1)
            new = kk_ref[q + 1, R] * center + kk_ref[q, R] * ((north + south) + (west + east))
            if step < 2 * STEPS:
                x_ref[R] = new
            else:
                for ct in range(2):
                    out_ref[pl.ds(row_at(R - HALO, ct), SUB, stride=64), :] = (
                        new[:, ct * LANES:(ct + 1) * LANES])
            north, center = center, south


def diffuse(view, nh, sh, pw, pe, cn, cs, adj, kk):
    groups = nh.shape[0]
    row_spec = pl.BlockSpec((1, HALO, 2, SUB, LANES), lambda g: (g, 0, 0, 0, 0))
    col_spec = pl.BlockSpec((1, 2, SUB, LANES), lambda g: (g, 0, 0, 0))
    corner_spec = pl.BlockSpec((1, SUB, LANES), lambda g: (g, 0, 0))
    tile_spec = pl.BlockSpec((512, LANES), lambda g: (g, 0))
    return pl.pallas_call(
        diffuse_kernel,
        grid=(groups,),
        out_shape=jax.ShapeDtypeStruct(view.shape, F32),
        in_specs=[tile_spec, row_spec, row_spec, col_spec, col_spec, corner_spec, corner_spec,
                  pl.BlockSpec(adj.shape, lambda g: (0, 0, 0)),
                  pl.BlockSpec(kk.shape, lambda g: (0, 0, 0, 0))],
        out_specs=tile_spec,
        scratch_shapes=[pltpu.VMEM(adj.shape, F32)],
        compiler_params=vmem(48),
        name="diffuse",
    )(view, nh, sh, pw, pe, cn, cs, adj, kk)


def shards(innovation, jacobian, channel_count, owner, footprint, weight, perturbation,
           scale_first, scale_second):
    members, levels, rows, cols = perturbation.shape
    n_lat, n_lon = lax.axis_size("lat"), lax.axis_size("lon")
    fields = members * levels
    obs = innovation.shape[1]
    view = perturbation.reshape(fields, rows // SUB, SUB, cols // LANES, LANES)
    view = view.transpose(0, 1, 3, 2, 4).reshape(fields * 64, LANES)

    north, south, west, east = edges(view, fields // SUB)
    down = [(i, i + 1) for i in range(n_lat - 1)]
    up = [(i + 1, i) for i in range(n_lat - 1)]
    right = [(i, (i + 1) % n_lon) for i in range(n_lon)]
    left = [((i + 1) % n_lon, i) for i in range(n_lon)]
    pe = lax.ppermute(west, "lon", left)
    pw = lax.ppermute(east, "lon", right)
    nh = lax.ppermute(south, "lat", down)
    sh = lax.ppermute(north, "lat", up)
    lane = lax.broadcasted_iota(I32, (1, SUB, LANES), 2)
    top = jnp.where(lane < 48, pw[:, 0], jnp.roll(pe[:, 0], 64, axis=2))
    bottom = jnp.where(lane >= 80, pw[:, 1], jnp.roll(pe[:, 1], 64, axis=2))
    cs = lax.ppermute(top, "lat", up)
    cn = lax.ppermute(bottom, "lat", down)

    windows = pack(innovation, jacobian, channel_count.reshape(1, obs), owner.reshape(1, obs),
                   footprint, weight)
    kap = jnp.stack([scale_first, 1.0 - 4.0 * scale_first, scale_second, 1.0 - 4.0 * scale_second],
                    axis=1)
    n = n_lat * n_lon
    got, kk = route(windows.reshape(n, 6, 4, LANES), kap, n_lat, n_lon)
    adjoint = total(got.reshape(n * 24, LANES), rows, cols)
    adj = widen(adjoint, n_lat, n_lon)
    out = diffuse(view, nh, sh, pw, pe, cn, cs, adj, kk)
    out = out.reshape(fields, rows // SUB, cols // LANES, SUB, LANES).transpose(0, 1, 3, 2, 4)
    return out.reshape(members, levels, rows, cols)


def solution(mesh):
    both = ("lat", "lon")
    return jax.shard_map(
        shards,
        mesh=mesh,
        in_specs=(
            P(None, both),
            P(None, None, both),
            P(both),
            P(both, None),
            P(None, both),
            P(None, both),
            P(None, None, "lat", "lon"),
            P("lat", "lon"),
            P("lat", "lon"),
        ),
        out_specs=P(None, None, "lat", "lon"),
        check_vma=False,
    )
```

```python
import jax
import jax.numpy as jnp
import numpy as np
from jax import lax
from jax.experimental import pallas as pl
from jax.experimental.pallas import tpu as pltpu
from jax.sharding import PartitionSpec as P

STEPS = 3
HALO = 2 * STEPS
LANES = 128
SUB = 8
MESH = pl.DeviceIdType.MESH
F32 = jnp.float32
BF16 = jnp.bfloat16
I32 = jnp.int32
NT = (((1,), (1,)), ((), ()))


def iota(shape, dim):
    return lax.broadcasted_iota(I32, shape, dim)


def dot(a, b):
    return jnp.dot(a, b, preferred_element_type=F32)


def dot_nt(a, b):
    return lax.dot_general(a, b, NT, preferred_element_type=F32)


def vmem(limit, **kw):
    return pltpu.CompilerParams(vmem_limit_bytes=limit << 20, **kw)


def row_at(r, ct):
    return (r // SUB) * 16 + ct * SUB + r % SUB


def edges_kernel(p_ref, n_ref, s_ref, w_ref, e_ref):
    group = iota((SUB, LANES), 1) // SUB

    def load(r, ct):
        return p_ref[pl.ds(row_at(r, ct), SUB, stride=64), :]

    for r in range(HALO):
        for ct in range(2):
            n_ref[0, r, ct] = load(r, ct)
            s_ref[0, r, ct] = load(32 - HALO + r, ct)
    for b in range(2):
        w = jnp.zeros((SUB, LANES), F32)
        e = jnp.zeros((SUB, LANES), F32)
        for j in range(16):
            w = jnp.where(group == j, pltpu.roll(load(16 * b + j, 0), 8 * j, 1), w)
            e = jnp.where(group == j, pltpu.roll(load(16 * b + j, 1), (8 * j + 8) % LANES, 1), e)
        w_ref[0, b] = w
        e_ref[0, b] = e


def edges(view, groups):
    rows = jax.ShapeDtypeStruct((groups, HALO, 2, SUB, LANES), F32)
    cols = jax.ShapeDtypeStruct((groups, 2, SUB, LANES), F32)
    row_spec = pl.BlockSpec((1, HALO, 2, SUB, LANES), lambda g: (g, 0, 0, 0, 0))
    col_spec = pl.BlockSpec((1, 2, SUB, LANES), lambda g: (g, 0, 0, 0))
    return pl.pallas_call(
        edges_kernel,
        grid=(groups,),
        out_shape=(rows, rows, cols, cols),
        in_specs=[pl.BlockSpec((512, LANES), lambda g: (g, 0))],
        out_specs=(row_spec, row_spec, col_spec, col_spec),
        compiler_params=vmem(32),
        name="edges",
    )(view)


def pack_kernel(inn_ref, jac_ref, cc_ref, own_ref, foot_ref, wgt_ref, out_ref,
                tot_ref, acc_ref, sorted_ref, cnt_v, cnt_s, sem):
    chans, obs = inn_ref.shape
    blk = 256
    ones = jnp.ones((2 * blk, LANES), BF16)
    ones8 = jnp.ones((SUB, 2 * blk), BF16)
    tot_ref[...] = jnp.zeros_like(tot_ref)

    def count(i, row):
        own = own_ref[:, pl.ds(pl.multiple_of(i * 2 * blk, 2 * blk), 2 * blk)]
        hot = (iota((LANES, 2 * blk), 0) == own).astype(F32).astype(BF16)
        tot_ref[...] += dot(hot, ones)
        return row + dot_nt(ones8, hot)

    tot_row = lax.fori_loop(0, obs // (2 * blk), count, jnp.zeros((SUB, LANES), F32))
    upper = (iota((LANES, LANES), 0) < iota((LANES, LANES), 1)).astype(F32).astype(BF16)
    lower = (iota((LANES, LANES), 0) > iota((LANES, LANES), 1)).astype(F32).astype(BF16)
    cnt_v[0:SUB] = dot(tot_row.astype(BF16), upper).astype(I32)
    cnt_v[SUB:2 * SUB] = tot_row.astype(I32)
    to_smem = pltpu.make_async_copy(cnt_v, cnt_s, sem)
    to_smem.start()
    tot_ref[...] = dot(lower, tot_ref[...].astype(BF16))
    upper_b = (iota((blk, blk), 0) < iota((blk, blk), 1)).astype(F32).astype(BF16)
    acc_ref[...] = jnp.zeros_like(acc_ref)

    def block(i, carry):
        at = pl.ds(pl.multiple_of(i * blk, blk), blk)
        own = own_ref[:, at]
        hot = iota((LANES, blk), 0) == own
        hot_b = hot.astype(F32).astype(BF16)
        base = tot_ref[...]
        place = dot(hot_b, upper_b) + jnp.concatenate([base, base], axis=1)
        tot_ref[...] = base + dot(hot_b, ones[:blk])
        pos = jnp.sum(jnp.where(hot, place, 0.0), axis=0, keepdims=True).astype(I32)
        cc = cc_ref[:, at]
        prof = jnp.zeros((4, blk), F32)
        for c in range(chans):
            live = jnp.where(cc > c, inn_ref[c:c + 1, at], 0.0)
            prof = prof + jac_ref[c, :, at] * live
        full = jnp.concatenate([wgt_ref[:, at], foot_ref[:, at].astype(F32), prof, prof], axis=0)
        head = full.astype(BF16).astype(F32)
        both = jnp.concatenate([head, full - head], axis=0)
        hi = lax.shift_right_logical(pos, 8)
        lo = lax.bitwise_and(pos, 255)
        spread = jnp.concatenate([jnp.where(hi == h, both, 0.0) for h in range(obs // blk)], axis=0)
        hot_lo = (iota((blk, blk), 0) == lo).astype(F32).astype(BF16)
        acc_ref[...] += dot_nt(spread.astype(BF16), hot_lo)
        return carry

    lax.fori_loop(0, obs // blk, block, 0)
    for h in range(obs // blk):
        s = acc_ref[48 * h:48 * h + 24, :] + acc_ref[48 * h + 24:48 * h + 48, :]
        sorted_ref[2 * h] = s[:, :LANES]
        sorted_ref[2 * h + 1] = s[:, LANES:]
    for t in range(2):
        sorted_ref[obs // LANES + t] = jnp.zeros((24, LANES), F32)
    to_smem.wait()
    lane = iota((24, LANES), 1)

    def window(i, carry):
        for u in range(4):
            d = i * 4 + u
            first = cnt_s[0, d]
            number = cnt_s[SUB, d]
            t = lax.shift_right_logical(first, 7)
            off = lax.bitwise_and(first, 127)
            y = jnp.where(lane >= off, sorted_ref[t], sorted_ref[t + 1])
            y = pltpu.roll(y, lax.bitwise_and(LANES - off, 127), 1)
            out_ref[pl.ds(pl.multiple_of(d * 24, 8), 24), :] = jnp.where(lane < number, y, 0.0)
        return carry

    lax.fori_loop(0, LANES // 4, window, 0)


def pack(inn, jac, cc, own, foot, wgt):
    obs = inn.shape[1]
    return pl.pallas_call(
        pack_kernel,
        out_shape=jax.ShapeDtypeStruct((24 * LANES, LANES), F32),
        in_specs=[pl.BlockSpec(memory_space=pltpu.VMEM)] * 6,
        out_specs=pl.BlockSpec(memory_space=pltpu.VMEM),
        scratch_shapes=[
            pltpu.VMEM((LANES, LANES), F32),
            pltpu.VMEM((48 * (obs // 256), 256), F32),
            pltpu.VMEM((obs // LANES + 2, 24, LANES), F32),
            pltpu.VMEM((2 * SUB, LANES), I32),
            pltpu.SMEM((2 * SUB, LANES), I32),
            pltpu.SemaphoreType.DMA,
        ],
        compiler_params=vmem(40),
        name="pack",
    )(inn, jac, cc, own, foot, wgt)


DIRS = ((1, 0), (-1, 0), (0, 1), (0, -1), (1, 1), (1, -1), (-1, 1), (-1, -1))


def halo_copies(src, mid, wb, eb, send, recv, n_lon):
    rows = src.shape[0]
    lat, lon = lax.axis_index("lat"), lax.axis_index("lon")
    copies = []
    for k, (dy, dx) in enumerate(DIRS):
        take = {1: pl.ds(rows - HALO, HALO), -1: pl.ds(0, HALO), 0: pl.ds(0, rows)}[dy]
        put = {1: pl.ds(0, HALO), -1: pl.ds(HALO + rows, HALO), 0: pl.ds(HALO, rows)}[dy]
        if dx == 0:
            s, d = src.at[take], mid.at[put]
        elif dx == 1:
            s, d = src.at[take, :, pl.ds(LANES, LANES)], wb.at[put]
        else:
            s, d = src.at[take, :, pl.ds(0, LANES)], eb.at[put]
        to = (lat + dy, lax.rem(lon + dx + n_lon, n_lon))
        copies.append(pltpu.make_async_remote_copy(
            src_ref=s, dst_ref=d, send_sem=send.at[k], recv_sem=recv.at[k],
            device_id=to, device_id_type=MESH))
    return copies


def when_lat(dy, lat, n_lat, fn):
    if dy == 0:
        fn()
    elif dy == 1:
        pl.when(lat < n_lat - 1)(fn)
    else:
        pl.when(lat > 0)(fn)


def halo_start(copies, lat, n_lat):
    for k, (dy, dx) in enumerate(DIRS):
        when_lat(dy, lat, n_lat, copies[k].start)


def halo_wait(copies, lat, n_lat):
    for k, (dy, dx) in enumerate(DIRS):
        when_lat(dy, lat, n_lat, copies[k].wait_send)
        when_lat(-dy, lat, n_lat, copies[k].wait_recv)


def halo_clear(mid, wb, eb, rows):
    for ref in (mid, wb, eb):
        for r in list(range(HALO)) + list(range(HALO + rows, 2 * HALO + rows)):
            ref[r] = jnp.zeros(ref.shape[1:], F32)


def lane_of(e):
    return (e % 3) * LANES + e // 3


def layouts():
    packed = np.zeros((4 * LANES, 3 * LANES), np.float32)
    whole = np.zeros((4 * LANES, 3 * LANES), np.float32)
    for c in range(2 * LANES):
        packed[c, lane_of(c + HALO)] = whole[c, lane_of(c + HALO)] = 1.0
    for q in range(LANES):
        if q % 8 >= 2:
            packed[2 * LANES + q, lane_of(q % 8 - 2)] = 1.0
        if q % 8 < HALO:
            packed[3 * LANES + q, lane_of(2 * LANES + HALO + q % 8)] = 1.0
    for q in range(HALO):
        whole[3 * LANES - HALO + q, lane_of(q)] = 1.0
        whole[3 * LANES + q, lane_of(2 * LANES + HALO + q)] = 1.0
    back = packed[:2 * LANES].T
    return [jnp.asarray(m, BF16) for m in (packed, whole, back)]


def parts(x, count):
    out = []
    for _ in range(count - 1):
        head = x.astype(BF16)
        out.append(head)
        x = x - head.astype(F32)
    return out + [x.astype(BF16)]


def moved(x, matrix, count):
    total = None
    for p in parts(x, count):
        y = dot(p, matrix)
        total = y if total is None else total + y
    return total


def interleaved(src, mid, wb, eb, whole, rows, start, count):
    lines = []
    for R in range(start, start + count):
        inner = src[R - HALO] if HALO <= R < HALO + rows else mid[R]
        lines.append(jnp.concatenate([inner, wb[R], eb[R]], axis=1))
    return moved(jnp.concatenate(lines, axis=0), whole, 3)


def route_kernel(n_lat, n_lon, s_ref, kap_ref, whole_ref, kk_ref, adj_ref,
                 got, acc, sums, mid, wb, eb, mid2, wb2, eb2,
                 send_sem, recv_sem, hs, hr, hs2, hr2):
    lat, lon = lax.axis_index("lat"), lax.axis_index("lon")
    n = n_lat * n_lon
    me = lat * n_lon + lon
    rows = kap_ref.shape[0]
    ext = rows + 2 * HALO
    groups = recv_sem.shape[0]
    per = n // groups
    halo_clear(mid, wb, eb, rows)
    halo_clear(mid2, wb2, eb2, rows)
    bar = pltpu.get_barrier_semaphore()

    def place(k):
        t = lax.rem(me + k, n)
        return t, (lax.div(t, n_lon), lax.rem(t, n_lon))

    def signal(k, c):
        pl.semaphore_signal(bar, inc=1, device_id=place(k)[1], device_id_type=MESH)
        return c

    lax.fori_loop(1, n, signal, 0)
    acc[...] = jnp.zeros_like(acc)
    pl.semaphore_wait(bar, n - 1)
    copies = halo_copies(kap_ref, mid, wb, eb, hs, hr, n_lon)
    halo_start(copies, lat, n_lat)
    for g in range(groups):
        def send(k, c, g=g):
            t, to = place(k)
            pltpu.make_async_remote_copy(
                src_ref=s_ref.at[t, pl.ds(0, 5)], dst_ref=got.at[k, pl.ds(0, 5)],
                send_sem=send_sem, recv_sem=recv_sem.at[g], device_id=to, device_id_type=MESH).start()
            return c

        lax.fori_loop(max(1, g * per), (g + 1) * per, send, 0)

    halo_wait(copies, lat, n_lat)
    for half in range(2):
        x = interleaved(kap_ref, mid, wb, eb, whole_ref[...], rows, half * ext // 2, ext // 2)
        for i in range(ext // 2):
            for q in range(4):
                line = x[4 * i + q:4 * i + q + 1]
                for t in range(3):
                    kk_ref[q, half * ext // 2 + i, t] = jnp.broadcast_to(
                        line[:, t * LANES:(t + 1) * LANES], (SUB, LANES))

    sub = iota((SUB, LANES), 0)
    row_ids = (iota((2 * LANES, LANES), 0) // SUB).astype(F32).astype(BF16)
    col_ids = iota((2 * LANES, LANES), 0).astype(F32).astype(BF16)

    def add(block):
        w = jnp.concatenate([block[0], block[1]], axis=0)
        cell = jnp.concatenate([block[2], block[3]], axis=0).astype(I32)
        prof = jnp.concatenate([block[4], block[4]], axis=0)
        cell_row = lax.shift_right_logical(cell, 8).astype(F32).astype(BF16)
        cell_col = lax.bitwise_and(cell, 255).astype(F32).astype(BF16)
        left, right = [], []
        for f in range(SUB):
            v = w[f:f + 1] * prof
            head = v.astype(BF16).astype(F32)
            both = jnp.where(sub < 4, head, v - head).astype(BF16)
            both = jnp.concatenate([both] * 32, axis=0)
            left.append(jnp.where(row_ids == cell_row[f:f + 1], both, jnp.zeros_like(both)))
            right.append(jnp.where(col_ids == cell_col[f:f + 1], jnp.ones_like(both), jnp.zeros_like(both)))
        acc[...] += dot_nt(jnp.concatenate(left, axis=1), jnp.concatenate(right, axis=1))

    add(s_ref[me])
    for g in range(groups):
        first, last = max(1, g * per), (g + 1) * per
        part = got.at[pl.ds(first, last - first), pl.ds(0, 5)]
        pltpu.make_async_remote_copy(
            src_ref=part, dst_ref=part, send_sem=send_sem, recv_sem=recv_sem.at[g],
            device_id=place(1)[1], device_id_type=MESH).wait_recv()

        def take(k, c):
            add(got[k])
            return c

        lax.fori_loop(first, last, take, 0)

    for r in range(rows):
        x = acc[SUB * r:SUB * r + SUB, :]
        sums[r] = (x + pltpu.roll(x, 4, 0))[0:4]
    copies = halo_copies(sums, mid2, wb2, eb2, hs2, hr2, n_lon)
    halo_start(copies, lat, n_lat)
    halo_wait(copies, lat, n_lat)
    x = interleaved(sums, mid2, wb2, eb2, whole_ref[...], rows, 0, ext)
    for R in range(ext):
        for t in range(3):
            v = x[4 * R:4 * R + 4, t * LANES:(t + 1) * LANES]
            adj_ref[R, t] = jnp.concatenate([v, v], axis=0)
    every = got.at[pl.ds(1, n - 1), pl.ds(0, 5)]
    pltpu.make_async_remote_copy(
        src_ref=every, dst_ref=every, send_sem=send_sem, recv_sem=recv_sem.at[0],
        device_id=place(1)[1], device_id_type=MESH).wait_send()


def route(windows, kap, whole, n_lat, n_lon):
    rows = kap.shape[0]
    ext = rows + 2 * HALO
    spec = pl.BlockSpec(memory_space=pltpu.VMEM)
    halo = [pltpu.VMEM((ext, 4, w * LANES), F32) for w in (2, 1, 1)]
    return pl.pallas_call(
        lambda *refs: route_kernel(n_lat, n_lon, *refs),
        out_shape=(jax.ShapeDtypeStruct((4, ext, 3, SUB, LANES), F32),
                   jax.ShapeDtypeStruct((ext, 3, SUB, LANES), F32)),
        in_specs=[spec] * 3,
        out_specs=(spec, spec),
        scratch_shapes=[
            pltpu.VMEM(windows.shape, F32),
            pltpu.VMEM((SUB * rows, 2 * LANES), F32),
            pltpu.VMEM((rows, 4, 2 * LANES), F32),
        ] + halo + halo + [
            pltpu.SemaphoreType.DMA, pltpu.SemaphoreType.DMA((8,)),
        ] + [pltpu.SemaphoreType.DMA((8,))] * 4,
        compiler_params=vmem(48, collective_id=0, has_side_effects=True),
        name="route",
    )(windows, kap, whole)


def diffuse_kernel(p_ref, nh_ref, sh_ref, pw_ref, pe_ref, cn_ref, cs_ref, adj_ref, kk_ref,
                   into_ref, back_ref, out_ref, x_ref):
    rows = 32
    ext = rows + 2 * HALO
    group = iota((SUB, LANES), 1) // SUB

    def lines(g, R):
        r = R - HALO
        if r < 0:
            mid = [nh_ref[g, R, ct] for ct in range(2)]
            w, w_at, e, e_at = cn_ref[g], 10 + R, cn_ref[g], 2 + R
        elif r >= rows:
            mid = [sh_ref[g, r - rows, ct] for ct in range(2)]
            w, w_at, e, e_at = cs_ref[g], r - rows, cs_ref[g], 8 + r - rows
        else:
            mid = [p_ref[pl.ds(512 * g + row_at(r, ct), SUB, stride=64), :] for ct in range(2)]
            w, w_at, e, e_at = pw_ref[g, r // 16], r % 16, pe_ref[g, r // 16], r % 16
        w = jnp.where(group == w_at, w, 0.0)
        e = jnp.where(group == e_at, e, 0.0)
        return jnp.concatenate(mid + [w, e], axis=1)

    for g in range(nh_ref.shape[0]):
        for start in range(0, ext, ext // 2):
            x = jnp.concatenate([lines(g, R) for R in range(start, start + ext // 2)], axis=0)
            x = moved(x, into_ref[...], 2)
            for i in range(ext // 2):
                for t in range(3):
                    x_ref[start + i, t] = (
                        x[SUB * i:SUB * i + SUB, t * LANES:(t + 1) * LANES] * adj_ref[start + i, t])
        for step in range(1, 2 * STEPS + 1):
            q = 0 if step <= STEPS else 2
            north = [x_ref[step - 1, t] for t in range(3)]
            center = [x_ref[step, t] for t in range(3)]
            for R in range(step, ext - step):
                south = [x_ref[R + 1, t] for t in range(3)]
                c0, c1, c2 = center
                sides = [pltpu.roll(c2, 1, 1) + c1, c0 + c2, c1 + pltpu.roll(c0, LANES - 1, 1)]
                for t in range(3):
                    x_ref[R, t] = (kk_ref[q + 1, R, t] * center[t]
                                   + kk_ref[q, R, t] * ((north[t] + south[t]) + sides[t]))
                north, center = center, south
        for start in range(0, rows, rows // 2):
            y = jnp.concatenate(
                [jnp.concatenate([x_ref[HALO + r, t] for t in range(3)], axis=1)
                 for r in range(start, start + rows // 2)], axis=0)
            y = moved(y, back_ref[...], 2)
            for i in range(rows // 2):
                for ct in range(2):
                    out_ref[pl.ds(512 * g + row_at(start + i, ct), SUB, stride=64), :] = (
                        y[SUB * i:SUB * i + SUB, ct * LANES:(ct + 1) * LANES])


def diffuse(view, nh, sh, pw, pe, cn, cs, adj, kk, into, back):
    groups = nh.shape[0]
    per = 2
    row_spec = pl.BlockSpec((per, HALO, 2, SUB, LANES), lambda g: (g, 0, 0, 0, 0))
    col_spec = pl.BlockSpec((per, 2, SUB, LANES), lambda g: (g, 0, 0, 0))
    corner_spec = pl.BlockSpec((per, SUB, LANES), lambda g: (g, 0, 0))
    tile_spec = pl.BlockSpec((per * 512, LANES), lambda g: (g, 0))
    fixed = [pl.BlockSpec(a.shape, lambda g, nd=a.ndim: (0,) * nd) for a in (adj, kk, into, back)]
    return pl.pallas_call(
        diffuse_kernel,
        grid=(groups // per,),
        out_shape=jax.ShapeDtypeStruct(view.shape, F32),
        in_specs=[tile_spec, row_spec, row_spec, col_spec, col_spec, corner_spec, corner_spec] + fixed,
        out_specs=tile_spec,
        scratch_shapes=[pltpu.VMEM(adj.shape, F32)],
        compiler_params=vmem(48),
        name="diffuse",
    )(view, nh, sh, pw, pe, cn, cs, adj, kk, into, back)


def shards(innovation, jacobian, channel_count, owner, footprint, weight, perturbation,
           scale_first, scale_second):
    members, levels, rows, cols = perturbation.shape
    n_lat, n_lon = lax.axis_size("lat"), lax.axis_size("lon")
    fields = members * levels
    obs = innovation.shape[1]
    view = perturbation.reshape(fields, rows // SUB, SUB, cols // LANES, LANES)
    view = view.transpose(0, 1, 3, 2, 4).reshape(fields * 64, LANES)

    north, south, west, east = edges(view, fields // SUB)
    down = [(i, i + 1) for i in range(n_lat - 1)]
    up = [(i + 1, i) for i in range(n_lat - 1)]
    right = [(i, (i + 1) % n_lon) for i in range(n_lon)]
    left = [((i + 1) % n_lon, i) for i in range(n_lon)]
    pe = lax.ppermute(west, "lon", left)
    pw = lax.ppermute(east, "lon", right)
    nh = lax.ppermute(south, "lat", down)
    sh = lax.ppermute(north, "lat", up)
    lane = lax.broadcasted_iota(I32, (1, SUB, LANES), 2)
    top = jnp.where(lane < 48, pw[:, 0], jnp.roll(pe[:, 0], 64, axis=2))
    bottom = jnp.where(lane >= 80, pw[:, 1], jnp.roll(pe[:, 1], 64, axis=2))
    cs = lax.ppermute(top, "lat", up)
    cn = lax.ppermute(bottom, "lat", down)

    windows = pack(innovation, jacobian, channel_count.reshape(1, obs), owner.reshape(1, obs),
                   footprint, weight)
    kap = jnp.stack([scale_first, 1.0 - 4.0 * scale_first, scale_second, 1.0 - 4.0 * scale_second],
                    axis=1)
    into, whole, back = layouts()
    kk, adj = route(windows.reshape(n_lat * n_lon, 6, 4, LANES), kap, whole, n_lat, n_lon)
    out = diffuse(view, nh, sh, pw, pe, cn, cs, adj, kk, into, back)
    out = out.reshape(fields, rows // SUB, cols // LANES, SUB, LANES).transpose(0, 1, 3, 2, 4)
    return out.reshape(members, levels, rows, cols)


def solution(mesh):
    both = ("lat", "lon")
    return jax.shard_map(
        shards,
        mesh=mesh,
        in_specs=(
            P(None, both),
            P(None, None, both),
            P(both),
            P(both, None),
            P(None, both),
            P(None, both),
            P(None, None, "lat", "lon"),
            P("lat", "lon"),
            P("lat", "lon"),
        ),
        out_specs=P(None, None, "lat", "lon"),
        check_vma=False,
    )
```

```python
import jax
import jax.numpy as jnp
import numpy as np
from jax import lax
from jax.experimental import pallas as pl
from jax.experimental.pallas import tpu as pltpu
from jax.sharding import PartitionSpec as P

STEPS = 3
HALO = 2 * STEPS
LANES = 128
SUB = 8
MESH = pl.DeviceIdType.MESH
F32 = jnp.float32
BF16 = jnp.bfloat16
I32 = jnp.int32
NT = (((1,), (1,)), ((), ()))


def iota(shape, dim):
    return lax.broadcasted_iota(I32, shape, dim)


def dot(a, b):
    return jnp.dot(a, b, preferred_element_type=F32)


def dot_nt(a, b):
    return lax.dot_general(a, b, NT, preferred_element_type=F32)


def vmem(limit, **kw):
    return pltpu.CompilerParams(vmem_limit_bytes=limit << 20, **kw)


def row_at(r, ct):
    return (r // SUB) * 16 + ct * SUB + r % SUB


def pack_kernel(inn_ref, jac_ref, cc_ref, own_ref, foot_ref, wgt_ref, out_ref,
                tot_ref, acc_ref, sorted_ref, cnt_v, cnt_s, sem):
    chans, obs = inn_ref.shape
    blk = 256
    ones = jnp.ones((2 * blk, LANES), BF16)
    ones8 = jnp.ones((SUB, 2 * blk), BF16)
    tot_ref[...] = jnp.zeros_like(tot_ref)

    def count(i, row):
        own = own_ref[:, pl.ds(pl.multiple_of(i * 2 * blk, 2 * blk), 2 * blk)]
        hot = (iota((LANES, 2 * blk), 0) == own).astype(F32).astype(BF16)
        tot_ref[...] += dot(hot, ones)
        return row + dot_nt(ones8, hot)

    tot_row = lax.fori_loop(0, obs // (2 * blk), count, jnp.zeros((SUB, LANES), F32))
    upper = (iota((LANES, LANES), 0) < iota((LANES, LANES), 1)).astype(F32).astype(BF16)
    lower = (iota((LANES, LANES), 0) > iota((LANES, LANES), 1)).astype(F32).astype(BF16)
    cnt_v[0:SUB] = dot(tot_row.astype(BF16), upper).astype(I32)
    cnt_v[SUB:2 * SUB] = tot_row.astype(I32)
    to_smem = pltpu.make_async_copy(cnt_v, cnt_s, sem)
    to_smem.start()
    tot_ref[...] = dot(lower, tot_ref[...].astype(BF16))
    upper_b = (iota((blk, blk), 0) < iota((blk, blk), 1)).astype(F32).astype(BF16)
    acc_ref[...] = jnp.zeros_like(acc_ref)

    def block(i, carry):
        at = pl.ds(pl.multiple_of(i * blk, blk), blk)
        own = own_ref[:, at]
        hot = iota((LANES, blk), 0) == own
        hot_b = hot.astype(F32).astype(BF16)
        base = tot_ref[...]
        place = dot(hot_b, upper_b) + jnp.concatenate([base, base], axis=1)
        tot_ref[...] = base + dot(hot_b, ones[:blk])
        pos = jnp.sum(jnp.where(hot, place, 0.0), axis=0, keepdims=True).astype(I32)
        cc = cc_ref[:, at]
        prof = jnp.zeros((4, blk), F32)
        for c in range(chans):
            live = jnp.where(cc > c, inn_ref[c:c + 1, at], 0.0)
            prof = prof + jac_ref[c, :, at] * live
        full = jnp.concatenate([wgt_ref[:, at], foot_ref[:, at].astype(F32), prof, prof], axis=0)
        head = full.astype(BF16).astype(F32)
        both = jnp.concatenate([head, full - head], axis=0)
        hi = lax.shift_right_logical(pos, 8)
        lo = lax.bitwise_and(pos, 255)
        spread = jnp.concatenate([jnp.where(hi == h, both, 0.0) for h in range(obs // blk)], axis=0)
        hot_lo = (iota((blk, blk), 0) == lo).astype(F32).astype(BF16)
        acc_ref[...] += dot_nt(spread.astype(BF16), hot_lo)
        return carry

    lax.fori_loop(0, obs // blk, block, 0)
    for h in range(obs // blk):
        s = acc_ref[48 * h:48 * h + 24, :] + acc_ref[48 * h + 24:48 * h + 48, :]
        sorted_ref[2 * h] = s[:, :LANES]
        sorted_ref[2 * h + 1] = s[:, LANES:]
    for t in range(2):
        sorted_ref[obs // LANES + t] = jnp.zeros((24, LANES), F32)
    to_smem.wait()
    lane = iota((24, LANES), 1)

    def window(i, carry):
        for u in range(4):
            d = i * 4 + u
            first = cnt_s[0, d]
            number = cnt_s[SUB, d]
            t = lax.shift_right_logical(first, 7)
            off = lax.bitwise_and(first, 127)
            y = jnp.where(lane >= off, sorted_ref[t], sorted_ref[t + 1])
            y = pltpu.roll(y, lax.bitwise_and(LANES - off, 127), 1)
            out_ref[pl.ds(pl.multiple_of(d * 24, 8), 24), :] = jnp.where(lane < number, y, 0.0)
        return carry

    lax.fori_loop(0, LANES // 4, window, 0)


def pack(inn, jac, cc, own, foot, wgt):
    obs = inn.shape[1]
    return pl.pallas_call(
        pack_kernel,
        out_shape=jax.ShapeDtypeStruct((24 * LANES, LANES), F32),
        in_specs=[pl.BlockSpec(memory_space=pltpu.VMEM)] * 6,
        out_specs=pl.BlockSpec(memory_space=pltpu.VMEM),
        scratch_shapes=[
            pltpu.VMEM((LANES, LANES), F32),
            pltpu.VMEM((48 * (obs // 256), 256), F32),
            pltpu.VMEM((obs // LANES + 2, 24, LANES), F32),
            pltpu.VMEM((2 * SUB, LANES), I32),
            pltpu.SMEM((2 * SUB, LANES), I32),
            pltpu.SemaphoreType.DMA,
        ],
        compiler_params=vmem(40),
        name="pack",
    )(inn, jac, cc, own, foot, wgt)


DIRS = ((1, 0), (-1, 0), (0, 1), (0, -1), (1, 1), (1, -1), (-1, 1), (-1, -1))


def halo_copies(src, mid, wb, eb, send, recv, n_lon):
    rows = src.shape[0]
    lat, lon = lax.axis_index("lat"), lax.axis_index("lon")
    copies = []
    for k, (dy, dx) in enumerate(DIRS):
        take = {1: pl.ds(rows - HALO, HALO), -1: pl.ds(0, HALO), 0: pl.ds(0, rows)}[dy]
        put = {1: pl.ds(0, HALO), -1: pl.ds(HALO + rows, HALO), 0: pl.ds(HALO, rows)}[dy]
        if dx == 0:
            s, d = src.at[take], mid.at[put]
        elif dx == 1:
            s, d = src.at[take, :, pl.ds(LANES, LANES)], wb.at[put]
        else:
            s, d = src.at[take, :, pl.ds(0, LANES)], eb.at[put]
        to = (lat + dy, lax.rem(lon + dx + n_lon, n_lon))
        copies.append(pltpu.make_async_remote_copy(
            src_ref=s, dst_ref=d, send_sem=send.at[k], recv_sem=recv.at[k],
            device_id=to, device_id_type=MESH))
    return copies


def when_lat(dy, lat, n_lat, fn):
    if dy == 0:
        fn()
    elif dy == 1:
        pl.when(lat < n_lat - 1)(fn)
    else:
        pl.when(lat > 0)(fn)


def halo_start(copies, lat, n_lat):
    for k, (dy, dx) in enumerate(DIRS):
        when_lat(dy, lat, n_lat, copies[k].start)


def halo_wait(copies, lat, n_lat):
    for k, (dy, dx) in enumerate(DIRS):
        when_lat(dy, lat, n_lat, copies[k].wait_send)
        when_lat(-dy, lat, n_lat, copies[k].wait_recv)


def halo_clear(mid, wb, eb, rows):
    for ref in (mid, wb, eb):
        for r in list(range(HALO)) + list(range(HALO + rows, 2 * HALO + rows)):
            ref[r] = jnp.zeros(ref.shape[1:], F32)


def lane_of(e):
    return (e % 3) * LANES + e // 3


def layouts():
    packed = np.zeros((4 * LANES, 3 * LANES), np.float32)
    whole = np.zeros((4 * LANES, 3 * LANES), np.float32)
    for c in range(2 * LANES):
        packed[c, lane_of(c + HALO)] = whole[c, lane_of(c + HALO)] = 1.0
    for q in range(LANES):
        if q % 8 >= 2:
            packed[2 * LANES + q, lane_of(q % 8 - 2)] = 1.0
        if q % 8 < HALO:
            packed[3 * LANES + q, lane_of(2 * LANES + HALO + q % 8)] = 1.0
    for q in range(HALO):
        whole[3 * LANES - HALO + q, lane_of(q)] = 1.0
        whole[3 * LANES + q, lane_of(2 * LANES + HALO + q)] = 1.0
    back = packed[:2 * LANES].T
    return [jnp.asarray(np.concatenate([m] * count), BF16)
            for m, count in ((whole, 3), (packed, 2), (back, 2))]


def moved(x, matrix, count):
    parts = []
    for _ in range(count - 1):
        head = x.astype(BF16)
        parts.append(head)
        x = x - head.astype(F32)
    return dot(jnp.concatenate(parts + [x.astype(BF16)], axis=1), matrix)


def interleaved(src, mid, wb, eb, whole, rows, start, count):
    lines = []
    for R in range(start, start + count):
        inner = src[R - HALO] if HALO <= R < HALO + rows else mid[R]
        lines.append(jnp.concatenate([inner, wb[R], eb[R]], axis=1))
    return moved(jnp.concatenate(lines, axis=0), whole, 3)


CHUNK = 4
BATCH = 8


def whole_kernel(n_lat, n_lon, s_ref, kap_ref, p_hbm, whole_ref, into_ref, back_ref, o_hbm,
                 pv, xi, nsend, ssend, nh, sh, wsend, esend, pw, pe, tsend, bsend, cs, cn, stage,
                 kk, adj, got, acc, sums, mid, wb, eb, mid2, wb2, eb2,
                 send_sem, recv_sem, hs, hr, hs2, hr2, row_s, row_r, col_s, col_r, cor_s, cor_r,
                 in_sem, out_sem):
    lat, lon = lax.axis_index("lat"), lax.axis_index("lon")
    n = n_lat * n_lon
    me = lat * n_lon + lon
    rows = kap_ref.shape[0]
    ext = rows + 2 * HALO
    fields8 = xi.shape[0]
    chunks = fields8 // CHUNK
    groups = recv_sem.shape[0]
    per = n // groups
    load = pltpu.make_async_copy(p_hbm, pv, in_sem)
    load.start()
    halo_clear(mid, wb, eb, rows)
    halo_clear(mid2, wb2, eb2, rows)
    bar = pltpu.get_barrier_semaphore()

    def place(k):
        t = lax.rem(me + k, n)
        return t, (lax.div(t, n_lon), lax.rem(t, n_lon))

    def signal(k, c):
        pl.semaphore_signal(bar, inc=1, device_id=place(k)[1], device_id_type=MESH)
        return c

    lax.fori_loop(1, n, signal, 0)

    @pl.when(lat == 0)
    def _():
        nh[...] = jnp.zeros_like(nh)
        cn[...] = jnp.zeros_like(cn)

    @pl.when(lat == n_lat - 1)
    def _():
        sh[...] = jnp.zeros_like(sh)
        cs[...] = jnp.zeros_like(cs)

    acc[...] = jnp.zeros_like(acc)
    pl.semaphore_wait(bar, n - 1)

    for g in range(groups):
        def send(k, c, g=g):
            t, to = place(k)
            pltpu.make_async_remote_copy(
                src_ref=s_ref.at[t, pl.ds(0, 5)], dst_ref=got.at[k, pl.ds(0, 5)],
                send_sem=send_sem, recv_sem=recv_sem.at[g], device_id=to, device_id_type=MESH).start()
            return c

        lax.fori_loop(max(1, g * per), (g + 1) * per, send, 0)
    kap_copies = halo_copies(kap_ref, mid, wb, eb, hs, hr, n_lon)
    halo_start(kap_copies, lat, n_lat)

    group = iota((SUB, LANES), 1) // SUB
    load.wait()

    def point(g, r, ct):
        return pv[pl.ds(512 * g + row_at(r, ct), SUB, stride=64), :]

    def edge(g, c):
        for r in range(HALO):
            for ct in range(2):
                nsend[g, r, ct] = point(g, r, ct)
                ssend[g, r, ct] = point(g, rows - HALO + r, ct)
        for b in range(2):
            w = jnp.zeros((SUB, LANES), F32)
            e = jnp.zeros((SUB, LANES), F32)
            for j in range(16):
                w = jnp.where(group == j, pltpu.roll(point(g, 16 * b + j, 0), 8 * j, 1), w)
                e = jnp.where(group == j, pltpu.roll(point(g, 16 * b + j, 1), (8 * j + 8) % LANES, 1), e)
            wsend[g, b] = w
            esend[g, b] = e
        return c

    lax.fori_loop(0, fields8, edge, 0)
    east, west = lax.rem(lon + 1, n_lon), lax.rem(lon + n_lon - 1, n_lon)

    def remote(src, dst, ss, rs, to):
        return pltpu.make_async_remote_copy(
            src_ref=src, dst_ref=dst, send_sem=ss, recv_sem=rs, device_id=to, device_id_type=MESH)

    cols = [remote(esend, pw, col_s.at[0], col_r.at[0], (lat, east)),
            remote(wsend, pe, col_s.at[1], col_r.at[1], (lat, west))]
    corners = [remote(bsend, cn, cor_s.at[0], cor_r.at[0], (lat + 1, lon)),
               remote(tsend, cs, cor_s.at[1], cor_r.at[1], (lat - 1, lon))]

    def row_copies(c):
        at = pl.ds(c * CHUNK, CHUNK)
        return [remote(ssend.at[at], nh.at[at], row_s.at[0, c], row_r.at[0, c], (lat + 1, lon)),
                remote(nsend.at[at], sh.at[at], row_s.at[1, c], row_r.at[1, c], (lat - 1, lon))]

    def start_rows(pair):
        pl.when(lat < n_lat - 1)(pair[0].start)
        pl.when(lat > 0)(pair[1].start)

    def wait_rows(pair):
        pl.when(lat < n_lat - 1)(pair[0].wait_send)
        pl.when(lat > 0)(pair[0].wait_recv)
        pl.when(lat > 0)(pair[1].wait_send)
        pl.when(lat < n_lat - 1)(pair[1].wait_recv)

    for copy in cols:
        copy.start()
    start_rows(row_copies(0))

    halo_wait(kap_copies, lat, n_lat)
    for half in range(2):
        x = interleaved(kap_ref, mid, wb, eb, whole_ref[...], rows, half * ext // 2, ext // 2)
        for i in range(ext // 2):
            for q in range(4):
                line = x[4 * i + q:4 * i + q + 1]
                for t in range(3):
                    kk[q, half * ext // 2 + i, t] = jnp.broadcast_to(
                        line[:, t * LANES:(t + 1) * LANES], (SUB, LANES))

    for copy in cols:
        copy.wait()

    def corner(g, c):
        tsend[g] = jnp.where(group < 6, pw[g, 0], pltpu.roll(pe[g, 0], 64, 1))
        bsend[g] = jnp.where(group >= 10, pw[g, 1], pltpu.roll(pe[g, 1], 64, 1))
        return c

    lax.fori_loop(0, fields8, corner, 0)
    start_rows(corners)

    def one(mid_rows, w, w_at, e, e_at):
        return jnp.concatenate(
            mid_rows + [jnp.where(group == w_at, w, 0.0), jnp.where(group == e_at, e, 0.0)], axis=1)

    def inner(g, c):
        x = jnp.concatenate(
            [one([point(g, r, 0), point(g, r, 1)], pw[g, r // 16], r % 16, pe[g, r // 16], r % 16)
             for r in range(rows)], axis=0)
        x = moved(x, into_ref[...], 2)
        for r in range(rows):
            for t in range(3):
                xi[g, HALO + r, t] = x[SUB * r:SUB * r + SUB, t * LANES:(t + 1) * LANES]
        return c

    lax.fori_loop(0, fields8, inner, 0)

    sub = iota((SUB, LANES), 0)
    row_ids = (iota((2 * LANES, LANES), 0) // SUB).astype(F32).astype(BF16)
    col_ids = iota((2 * LANES, LANES), 0).astype(F32).astype(BF16)

    def spread(block):
        w = jnp.concatenate([block[0], block[1]], axis=0)
        cell = jnp.concatenate([block[2], block[3]], axis=0).astype(I32)
        prof = jnp.concatenate([block[4], block[4]], axis=0)
        cell_row = lax.shift_right_logical(cell, 8).astype(F32).astype(BF16)
        cell_col = lax.bitwise_and(cell, 255).astype(F32).astype(BF16)
        left, right = [], []
        for f in range(SUB):
            v = w[f:f + 1] * prof
            head = v.astype(BF16).astype(F32)
            both = jnp.where(sub < 4, head, v - head).astype(BF16)
            both = jnp.concatenate([both] * 32, axis=0)
            left.append(jnp.where(row_ids == cell_row[f:f + 1], both, jnp.zeros_like(both)))
            right.append(jnp.where(col_ids == cell_col[f:f + 1], jnp.ones_like(both), jnp.zeros_like(both)))
        return left, right

    got[0] = s_ref[me]

    def add(i, c):
        left, right = [], []
        for u in range(BATCH):
            a, b = spread(got[i * BATCH + u])
            left += a
            right += b
        acc[...] += dot_nt(jnp.concatenate(left, axis=1), jnp.concatenate(right, axis=1))
        return c

    when_sent = {2: [1], 4: [2], 6: [3, 4]}
    for g in range(groups):
        first, last = max(1, g * per), (g + 1) * per
        part = got.at[pl.ds(first, last - first), pl.ds(0, 5)]
        remote(part, part, send_sem, recv_sem.at[g], place(1)[1]).wait_recv()
        for c in when_sent.get(g, []):
            start_rows(row_copies(c))
        lax.fori_loop(g * per // BATCH, (g + 1) * per // BATCH, add, 0)

    for r in range(rows):
        x = acc[SUB * r:SUB * r + SUB, :]
        sums[r] = (x + pltpu.roll(x, 4, 0))[0:4]
    copies = halo_copies(sums, mid2, wb2, eb2, hs2, hr2, n_lon)
    halo_start(copies, lat, n_lat)
    halo_wait(copies, lat, n_lat)
    x = interleaved(sums, mid2, wb2, eb2, whole_ref[...], rows, 0, ext)
    for R in range(ext):
        for t in range(3):
            v = x[4 * R:4 * R + 4, t * LANES:(t + 1) * LANES]
            adj[R, t] = jnp.concatenate([v, v], axis=0)

    wait_rows(corners)

    def out_copy(g):
        slot = lax.rem(g, 2)
        return pltpu.make_async_copy(
            stage.at[slot], o_hbm.at[pl.ds(512 * g, 512)], out_sem.at[slot])

    def diffuse(g, c):
        lines = [one([nh[g, j, 0], nh[g, j, 1]], cn[g], 10 + j, cn[g], 2 + j) for j in range(HALO)]
        lines += [one([sh[g, j, 0], sh[g, j, 1]], cs[g], j, cs[g], 8 + j) for j in range(HALO)]
        x = moved(jnp.concatenate(lines, axis=0), into_ref[...], 2)
        for j in range(2 * HALO):
            R = j if j < HALO else rows + j
            for t in range(3):
                xi[g, R, t] = x[SUB * j:SUB * j + SUB, t * LANES:(t + 1) * LANES] * adj[R, t]
        for R in range(HALO, HALO + rows):
            for t in range(3):
                xi[g, R, t] = xi[g, R, t] * adj[R, t]
        for step in range(1, 2 * STEPS + 1):
            q = 0 if step <= STEPS else 2
            north = [xi[g, step - 1, t] for t in range(3)]
            center = [xi[g, step, t] for t in range(3)]
            for R in range(step, ext - step):
                south = [xi[g, R + 1, t] for t in range(3)]
                c0, c1, c2 = center
                sides = [pltpu.roll(c2, 1, 1) + c1, c0 + c2, c1 + pltpu.roll(c0, LANES - 1, 1)]
                for t in range(3):
                    xi[g, R, t] = (kk[q + 1, R, t] * center[t]
                                   + kk[q, R, t] * ((north[t] + south[t]) + sides[t]))
                north, center = center, south
        pl.when(g >= 2)(lambda: out_copy(g - 2).wait())
        slot = lax.rem(g, 2)
        y = jnp.concatenate(
            [jnp.concatenate([xi[g, HALO + r, t] for t in range(3)], axis=1) for r in range(rows)],
            axis=0)
        y = moved(y, back_ref[...], 2)
        for r in range(rows):
            for ct in range(2):
                stage[slot, pl.ds(row_at(r, ct), SUB, stride=64), :] = (
                    y[SUB * r:SUB * r + SUB, ct * LANES:(ct + 1) * LANES])
        out_copy(g).start()
        return c

    def chunk(c, carry):
        wait_rows(row_copies(c))
        lax.fori_loop(c * CHUNK, (c + 1) * CHUNK, diffuse, 0)
        return carry

    lax.fori_loop(0, chunks, chunk, 0)
    out_copy(fields8 - 2).wait()
    out_copy(fields8 - 1).wait()
    every = got.at[pl.ds(1, n - 1), pl.ds(0, 5)]
    remote(every, every, send_sem, recv_sem.at[0], place(1)[1]).wait_send()


def whole(windows, kap, view, mats, n_lat, n_lon):
    rows = kap.shape[0]
    ext = rows + 2 * HALO
    g = view.shape[0] // 512
    spec = pl.BlockSpec(memory_space=pltpu.VMEM)
    hbm = pl.BlockSpec(memory_space=pl.ANY)
    halo = [pltpu.VMEM((ext, 4, w * LANES), F32) for w in (2, 1, 1)]
    dma = pltpu.SemaphoreType.DMA
    return pl.pallas_call(
        lambda *refs: whole_kernel(n_lat, n_lon, *refs),
        out_shape=jax.ShapeDtypeStruct(view.shape, F32),
        in_specs=[spec, spec, hbm] + [spec] * 3,
        out_specs=hbm,
        scratch_shapes=[
            pltpu.VMEM(view.shape, F32),
            pltpu.VMEM((g, ext, 3, SUB, LANES), F32),
        ] + [pltpu.VMEM((g, HALO, 2, SUB, LANES), F32)] * 4
        + [pltpu.VMEM((g, 2, SUB, LANES), F32)] * 4
        + [pltpu.VMEM((g, SUB, LANES), F32)] * 4 + [
            pltpu.VMEM((2, 512, LANES), F32),
            pltpu.VMEM((4, ext, 3, SUB, LANES), F32),
            pltpu.VMEM((ext, 3, SUB, LANES), F32),
            pltpu.VMEM(windows.shape, F32),
            pltpu.VMEM((SUB * rows, 2 * LANES), F32),
            pltpu.VMEM((rows, 4, 2 * LANES), F32),
        ] + halo + halo + [dma, dma((8,))] + [dma((8,))] * 4
        + [dma((2, g // CHUNK))] * 2 + [dma((2,))] * 4 + [dma, dma((2,))],
        compiler_params=vmem(60, collective_id=0, has_side_effects=True),
        name="whole",
    )(windows, kap, view, *mats)


def shards(innovation, jacobian, channel_count, owner, footprint, weight, perturbation,
           scale_first, scale_second):
    members, levels, rows, cols = perturbation.shape
    n_lat, n_lon = lax.axis_size("lat"), lax.axis_size("lon")
    fields = members * levels
    obs = innovation.shape[1]
    view = perturbation.reshape(fields, rows // SUB, SUB, cols // LANES, LANES)
    view = view.transpose(0, 1, 3, 2, 4).reshape(fields * 64, LANES)

    windows = pack(innovation, jacobian, channel_count.reshape(1, obs), owner.reshape(1, obs),
                   footprint, weight)
    kap = jnp.stack([scale_first, 1.0 - 4.0 * scale_first, scale_second, 1.0 - 4.0 * scale_second],
                    axis=1)
    out = whole(windows.reshape(n_lat * n_lon, 6, 4, LANES), kap, view, layouts(), n_lat, n_lon)
    out = out.reshape(fields, rows // SUB, cols // LANES, SUB, LANES).transpose(0, 1, 3, 2, 4)
    return out.reshape(members, levels, rows, cols)


def solution(mesh):
    both = ("lat", "lon")
    return jax.shard_map(
        shards,
        mesh=mesh,
        in_specs=(
            P(None, both),
            P(None, None, both),
            P(both),
            P(both, None),
            P(None, both),
            P(None, both),
            P(None, None, "lat", "lon"),
            P("lat", "lon"),
            P("lat", "lon"),
        ),
        out_specs=P(None, None, "lat", "lon"),
        check_vma=False,
    )
```

```python
import jax
import jax.numpy as jnp
import numpy as np
from jax import lax
from jax.experimental import pallas as pl
from jax.experimental.pallas import tpu as pltpu
from jax.sharding import PartitionSpec as P

STEPS = 3
HALO = 2 * STEPS
LANES = 128
SUB = 8
MESH = pl.DeviceIdType.MESH
F32 = jnp.float32
BF16 = jnp.bfloat16
I32 = jnp.int32
NT = (((1,), (1,)), ((), ()))


def iota(shape, dim):
    return lax.broadcasted_iota(I32, shape, dim)


def dot(a, b):
    return jnp.dot(a, b, preferred_element_type=F32)


def dot_nt(a, b):
    return lax.dot_general(a, b, NT, preferred_element_type=F32)


def vmem(limit, **kw):
    return pltpu.CompilerParams(vmem_limit_bytes=limit << 20, **kw)


def row_at(r, ct):
    return (r // SUB) * 16 + ct * SUB + r % SUB


def pack_kernel(inn_h, jac_h, cc_h, own_h, foot_h, wgt_h, out_ref,
                inn_ref, jac_ref, cc_ref, own_ref, foot_ref, wgt_ref,
                tot_ref, acc_ref, sorted_ref, cnt_v, cnt_s, sem, in_sem):
    chans, obs = inn_ref.shape
    blk = 256
    wide = 4 * blk
    loads = [pltpu.make_async_copy(h, v, in_sem.at[i]) for i, (h, v) in enumerate((
        (own_h, own_ref), (inn_h, inn_ref), (jac_h, jac_ref), (cc_h, cc_ref),
        (foot_h, foot_ref), (wgt_h, wgt_ref)))]
    for copy in loads:
        copy.start()
    loads[0].wait()
    hot_all = (iota((LANES, obs), 0) == own_ref[...]).astype(F32).astype(BF16)
    totals = dot(hot_all, jnp.ones((obs, LANES), BF16))
    tot_row = dot_nt(jnp.ones((SUB, obs), BF16), hot_all)
    upper = (iota((LANES, LANES), 0) < iota((LANES, LANES), 1)).astype(F32).astype(BF16)
    lower = (iota((LANES, LANES), 0) > iota((LANES, LANES), 1)).astype(F32).astype(BF16)
    cnt_v[0:SUB] = dot(tot_row.astype(BF16), upper).astype(I32)
    cnt_v[SUB:2 * SUB] = tot_row.astype(I32)
    to_smem = pltpu.make_async_copy(cnt_v, cnt_s, sem)
    to_smem.start()
    tot_ref[...] = dot(lower, totals.astype(BF16))
    upper_b = (iota((blk, blk), 0) < iota((blk, blk), 1)).astype(F32).astype(BF16)
    acc_ref[...] = jnp.zeros_like(acc_ref)
    for copy in loads[1:]:
        copy.wait()

    def block(i, carry):
        at = pl.ds(pl.multiple_of(i * wide, wide), wide)
        own = own_ref[:, at]
        hots = [iota((LANES, blk), 0) == own[:, j * blk:(j + 1) * blk] for j in range(4)]
        stack = jnp.concatenate([h.astype(F32).astype(BF16) for h in hots], axis=0)
        ranks = dot(stack, upper_b)
        sums = dot(stack, jnp.ones((blk, LANES), BF16))
        base = tot_ref[...]
        places = []
        for j in range(4):
            rank = ranks[LANES * j:LANES * (j + 1)] + jnp.concatenate([base, base], axis=1)
            places.append(jnp.sum(jnp.where(hots[j], rank, 0.0), axis=0, keepdims=True))
            base = base + sums[LANES * j:LANES * (j + 1)]
        tot_ref[...] = base
        pos = jnp.concatenate(places, axis=1).astype(I32)
        cc = cc_ref[:, at]
        prof = jnp.zeros((4, wide), F32)
        for c in range(chans):
            live = jnp.where(cc > c, inn_ref[c:c + 1, at], 0.0)
            prof = prof + jac_ref[c, :, at] * live
        full = jnp.concatenate([wgt_ref[:, at], foot_ref[:, at].astype(F32), prof, prof], axis=0)
        head = full.astype(BF16).astype(F32)
        both = jnp.concatenate([head, full - head], axis=0)
        hi = lax.shift_right_logical(pos, 8)
        lo = lax.bitwise_and(pos, 255)
        spread = jnp.concatenate(
            [jnp.where(hi == h, both, 0.0).astype(BF16) for h in range(obs // blk)], axis=0)
        hot_lo = (iota((blk, wide), 0) == lo).astype(F32).astype(BF16)
        acc_ref[...] += dot_nt(spread, hot_lo)
        return carry

    lax.fori_loop(0, obs // wide, block, 0)
    for h in range(obs // blk):
        s = acc_ref[48 * h:48 * h + 24, :] + acc_ref[48 * h + 24:48 * h + 48, :]
        sorted_ref[2 * h] = s[:, :LANES]
        sorted_ref[2 * h + 1] = s[:, LANES:]
    for t in range(2):
        sorted_ref[obs // LANES + t] = jnp.zeros((24, LANES), F32)
    to_smem.wait()
    lane = iota((24, LANES), 1)

    def window(i, carry):
        for u in range(4):
            d = i * 4 + u
            first = cnt_s[0, d]
            number = cnt_s[SUB, d]
            t = lax.shift_right_logical(first, 7)
            off = lax.bitwise_and(first, 127)
            y = jnp.where(lane >= off, sorted_ref[t], sorted_ref[t + 1])
            y = pltpu.roll(y, lax.bitwise_and(LANES - off, 127), 1)
            out_ref[pl.ds(pl.multiple_of(d * 24, 8), 24), :] = jnp.where(lane < number, y, 0.0)
        return carry

    lax.fori_loop(0, LANES // 4, window, 0)


def pack(inn, jac, cc, own, foot, wgt):
    obs = inn.shape[1]
    return pl.pallas_call(
        pack_kernel,
        out_shape=jax.ShapeDtypeStruct((24 * LANES, LANES), F32),
        in_specs=[pl.BlockSpec(memory_space=pl.ANY)] * 6,
        out_specs=pl.BlockSpec(memory_space=pltpu.VMEM),
        scratch_shapes=[pltpu.VMEM(a.shape, a.dtype) for a in (inn, jac, cc, own, foot, wgt)] + [
            pltpu.VMEM((LANES, LANES), F32),
            pltpu.VMEM((48 * (obs // 256), 256), F32),
            pltpu.VMEM((obs // LANES + 2, 24, LANES), F32),
            pltpu.VMEM((2 * SUB, LANES), I32),
            pltpu.SMEM((2 * SUB, LANES), I32),
            pltpu.SemaphoreType.DMA,
            pltpu.SemaphoreType.DMA((6,)),
        ],
        compiler_params=vmem(60),
        name="pack",
    )(inn, jac, cc, own, foot, wgt)


DIRS = ((1, 0), (-1, 0), (0, 1), (0, -1), (1, 1), (1, -1), (-1, 1), (-1, -1))


def halo_copies(src, mid, wb, eb, send, recv, n_lon):
    rows = src.shape[0]
    lat, lon = lax.axis_index("lat"), lax.axis_index("lon")
    copies = []
    for k, (dy, dx) in enumerate(DIRS):
        take = {1: pl.ds(rows - HALO, HALO), -1: pl.ds(0, HALO), 0: pl.ds(0, rows)}[dy]
        put = {1: pl.ds(0, HALO), -1: pl.ds(HALO + rows, HALO), 0: pl.ds(HALO, rows)}[dy]
        if dx == 0:
            s, d = src.at[take], mid.at[put]
        elif dx == 1:
            s, d = src.at[take, :, pl.ds(LANES, LANES)], wb.at[put]
        else:
            s, d = src.at[take, :, pl.ds(0, LANES)], eb.at[put]
        to = (lat + dy, lax.rem(lon + dx + n_lon, n_lon))
        copies.append(pltpu.make_async_remote_copy(
            src_ref=s, dst_ref=d, send_sem=send.at[k], recv_sem=recv.at[k],
            device_id=to, device_id_type=MESH))
    return copies


def when_lat(dy, lat, n_lat, fn):
    if dy == 0:
        fn()
    elif dy == 1:
        pl.when(lat < n_lat - 1)(fn)
    else:
        pl.when(lat > 0)(fn)


def halo_start(copies, lat, n_lat):
    for k, (dy, dx) in enumerate(DIRS):
        when_lat(dy, lat, n_lat, copies[k].start)


def halo_wait(copies, lat, n_lat):
    for k, (dy, dx) in enumerate(DIRS):
        when_lat(dy, lat, n_lat, copies[k].wait_send)
        when_lat(-dy, lat, n_lat, copies[k].wait_recv)


def halo_clear(mid, wb, eb, rows):
    for ref in (mid, wb, eb):
        for r in list(range(HALO)) + list(range(HALO + rows, 2 * HALO + rows)):
            ref[r] = jnp.zeros(ref.shape[1:], F32)


def lane_of(e):
    return (e % 3) * LANES + e // 3


def layouts():
    packed = np.zeros((4 * LANES, 3 * LANES), np.float32)
    whole = np.zeros((4 * LANES, 3 * LANES), np.float32)
    for c in range(2 * LANES):
        packed[c, lane_of(c + HALO)] = whole[c, lane_of(c + HALO)] = 1.0
    for q in range(LANES):
        if q % 8 >= 2:
            packed[2 * LANES + q, lane_of(q % 8 - 2)] = 1.0
        if q % 8 < HALO:
            packed[3 * LANES + q, lane_of(2 * LANES + HALO + q % 8)] = 1.0
    for q in range(HALO):
        whole[3 * LANES - HALO + q, lane_of(q)] = 1.0
        whole[3 * LANES + q, lane_of(2 * LANES + HALO + q)] = 1.0
    back = packed[:2 * LANES].T
    return [jnp.asarray(np.concatenate([m] * count), BF16)
            for m, count in ((whole, 3), (packed, 2), (back, 2))]


def moved(x, matrix, count):
    parts = []
    for _ in range(count - 1):
        head = x.astype(BF16)
        parts.append(head)
        x = x - head.astype(F32)
    return dot(jnp.concatenate(parts + [x.astype(BF16)], axis=1), matrix)


def interleaved(src, mid, wb, eb, whole, rows, start, count):
    lines = []
    for R in range(start, start + count):
        inner = src[R - HALO] if HALO <= R < HALO + rows else mid[R]
        lines.append(jnp.concatenate([inner, wb[R], eb[R]], axis=1))
    return moved(jnp.concatenate(lines, axis=0), whole, 3)


CHUNK = 4
BATCH = 8


def whole_kernel(n_lat, n_lon, s_ref, k1_ref, k2_ref, p_hbm, whole_ref, into_ref, o_hbm,
                 kap_ref, pv, xi, nsend, ssend, nh, sh, wsend, esend, pw, pe, tsend, bsend, cs, cn,
                 kk, adj, got, acc, sums, mid, wb, eb, mid2, wb2, eb2,
                 send_sem, recv_sem, hs, hr, hs2, hr2, row_s, row_r, col_s, col_r, cor_s, cor_r,
                 in_sem, out_sem):
    lat, lon = lax.axis_index("lat"), lax.axis_index("lon")
    n = n_lat * n_lon
    me = lat * n_lon + lon
    rows = kap_ref.shape[0]
    ext = rows + 2 * HALO
    fields8 = xi.shape[0]
    chunks = fields8 // CHUNK
    groups = recv_sem.shape[0]
    per = n // groups
    load = pltpu.make_async_copy(p_hbm, pv, in_sem)
    load.start()
    halo_clear(mid, wb, eb, rows)
    halo_clear(mid2, wb2, eb2, rows)
    bar = pltpu.get_barrier_semaphore()

    def place(k):
        t = lax.rem(me + k, n)
        return t, (lax.div(t, n_lon), lax.rem(t, n_lon))

    def signal(k, c):
        pl.semaphore_signal(bar, inc=1, device_id=place(k)[1], device_id_type=MESH)
        return c

    lax.fori_loop(1, n, signal, 0)
    for r in range(rows):
        k1, k2 = k1_ref[r:r + 1, :], k2_ref[r:r + 1, :]
        kap_ref[r] = jnp.concatenate([k1, 1.0 - 4.0 * k1, k2, 1.0 - 4.0 * k2], axis=0)

    @pl.when(lat == 0)
    def _():
        nh[...] = jnp.zeros_like(nh)
        cn[...] = jnp.zeros_like(cn)

    @pl.when(lat == n_lat - 1)
    def _():
        sh[...] = jnp.zeros_like(sh)
        cs[...] = jnp.zeros_like(cs)

    acc[...] = jnp.zeros_like(acc)
    pl.semaphore_wait(bar, n - 1)

    for g in range(groups):
        def send(k, c, g=g):
            t, to = place(k)
            pltpu.make_async_remote_copy(
                src_ref=s_ref.at[t, pl.ds(0, 5)], dst_ref=got.at[k, pl.ds(0, 5)],
                send_sem=send_sem, recv_sem=recv_sem.at[g], device_id=to, device_id_type=MESH).start()
            return c

        lax.fori_loop(max(1, g * per), (g + 1) * per, send, 0)
    kap_copies = halo_copies(kap_ref, mid, wb, eb, hs, hr, n_lon)
    halo_start(kap_copies, lat, n_lat)

    group = iota((SUB, LANES), 1) // SUB
    load.wait()

    def point(g, r, ct):
        return pv[pl.ds(512 * g + row_at(r, ct), SUB, stride=64), :]

    def edge(g, c):
        for r in range(HALO):
            for ct in range(2):
                nsend[g, r, ct] = point(g, r, ct)
                ssend[g, r, ct] = point(g, rows - HALO + r, ct)
        for b in range(2):
            w = jnp.zeros((SUB, LANES), F32)
            e = jnp.zeros((SUB, LANES), F32)
            for j in range(16):
                w = jnp.where(group == j, pltpu.roll(point(g, 16 * b + j, 0), 8 * j, 1), w)
                e = jnp.where(group == j, pltpu.roll(point(g, 16 * b + j, 1), (8 * j + 8) % LANES, 1), e)
            wsend[g, b] = w
            esend[g, b] = e
        return c

    lax.fori_loop(0, fields8, edge, 0)
    east, west = lax.rem(lon + 1, n_lon), lax.rem(lon + n_lon - 1, n_lon)

    def remote(src, dst, ss, rs, to):
        return pltpu.make_async_remote_copy(
            src_ref=src, dst_ref=dst, send_sem=ss, recv_sem=rs, device_id=to, device_id_type=MESH)

    cols = [remote(esend, pw, col_s.at[0], col_r.at[0], (lat, east)),
            remote(wsend, pe, col_s.at[1], col_r.at[1], (lat, west))]
    corners = [remote(bsend, cn, cor_s.at[0], cor_r.at[0], (lat + 1, lon)),
               remote(tsend, cs, cor_s.at[1], cor_r.at[1], (lat - 1, lon))]

    def row_copies(c):
        at = pl.ds(c * CHUNK, CHUNK)
        return [remote(ssend.at[at], nh.at[at], row_s.at[0, c], row_r.at[0, c], (lat + 1, lon)),
                remote(nsend.at[at], sh.at[at], row_s.at[1, c], row_r.at[1, c], (lat - 1, lon))]

    def start_rows(pair):
        pl.when(lat < n_lat - 1)(pair[0].start)
        pl.when(lat > 0)(pair[1].start)

    def wait_rows(pair):
        pl.when(lat < n_lat - 1)(pair[0].wait_send)
        pl.when(lat > 0)(pair[0].wait_recv)
        pl.when(lat > 0)(pair[1].wait_send)
        pl.when(lat < n_lat - 1)(pair[1].wait_recv)

    for copy in cols:
        copy.start()
    start_rows(row_copies(0))

    halo_wait(kap_copies, lat, n_lat)
    for half in range(2):
        x = interleaved(kap_ref, mid, wb, eb, whole_ref[...], rows, half * ext // 2, ext // 2)
        for i in range(ext // 2):
            for q in range(4):
                line = x[4 * i + q:4 * i + q + 1]
                for t in range(3):
                    kk[q, half * ext // 2 + i, t] = jnp.broadcast_to(
                        line[:, t * LANES:(t + 1) * LANES], (SUB, LANES))

    for copy in cols:
        copy.wait()

    def corner(g, c):
        tsend[g] = jnp.where(group < 6, pw[g, 0], pltpu.roll(pe[g, 0], 64, 1))
        bsend[g] = jnp.where(group >= 10, pw[g, 1], pltpu.roll(pe[g, 1], 64, 1))
        return c

    lax.fori_loop(0, fields8, corner, 0)
    start_rows(corners)

    def one(mid_rows, w, w_at, e, e_at):
        return jnp.concatenate(
            mid_rows + [jnp.where(group == w_at, w, 0.0), jnp.where(group == e_at, e, 0.0)], axis=1)

    def inner(c, carry):
        x = jnp.concatenate(
            [one([point(c * CHUNK + u, r, 0), point(c * CHUNK + u, r, 1)],
                 pw[c * CHUNK + u, r // 16], r % 16, pe[c * CHUNK + u, r // 16], r % 16)
             for u in range(CHUNK) for r in range(rows)], axis=0)
        x = moved(x, into_ref[...], 2)
        for u in range(CHUNK):
            for r in range(rows):
                i = SUB * (u * rows + r)
                for t in range(3):
                    xi[c * CHUNK + u, HALO + r, t] = x[i:i + SUB, t * LANES:(t + 1) * LANES]
        return carry

    for c in range(1, 3):
        start_rows(row_copies(c))
    lax.fori_loop(0, chunks, inner, 0)

    sub = iota((SUB, LANES), 0)
    row_ids = (iota((2 * LANES, LANES), 0) // SUB).astype(F32).astype(BF16)
    col_ids = iota((2 * LANES, LANES), 0).astype(F32).astype(BF16)

    def spread(block):
        w = jnp.concatenate([block[0], block[1]], axis=0)
        cell = jnp.concatenate([block[2], block[3]], axis=0).astype(I32)
        prof = jnp.concatenate([block[4], block[4]], axis=0)
        cell_row = lax.shift_right_logical(cell, 8).astype(F32).astype(BF16)
        cell_col = lax.bitwise_and(cell, 255).astype(F32).astype(BF16)
        left, right = [], []
        for f in range(SUB):
            v = w[f:f + 1] * prof
            head = v.astype(BF16).astype(F32)
            both = jnp.where(sub < 4, head, v - head).astype(BF16)
            both = jnp.concatenate([both] * 32, axis=0)
            left.append(jnp.where(row_ids == cell_row[f:f + 1], both, jnp.zeros_like(both)))
            right.append(jnp.where(col_ids == cell_col[f:f + 1], jnp.ones_like(both), jnp.zeros_like(both)))
        return left, right

    got[0] = s_ref[me]

    def add(i, c):
        left, right = [], []
        for u in range(BATCH):
            a, b = spread(got[i * BATCH + u])
            left += a
            right += b
        acc[...] += dot_nt(jnp.concatenate(left, axis=1), jnp.concatenate(right, axis=1))
        return c

    when_sent = {0: [3], 1: [4]}
    for g in range(groups):
        first, last = max(1, g * per), (g + 1) * per
        part = got.at[pl.ds(first, last - first), pl.ds(0, 5)]
        remote(part, part, send_sem, recv_sem.at[g], place(1)[1]).wait_recv()
        for c in when_sent.get(g, []):
            start_rows(row_copies(c))
        lax.fori_loop(g * per // BATCH, (g + 1) * per // BATCH, add, 0)

    for r in range(rows):
        x = acc[SUB * r:SUB * r + SUB, :]
        sums[r] = (x + pltpu.roll(x, 4, 0))[0:4]
    copies = halo_copies(sums, mid2, wb2, eb2, hs2, hr2, n_lon)
    halo_start(copies, lat, n_lat)
    halo_wait(copies, lat, n_lat)
    x = interleaved(sums, mid2, wb2, eb2, whole_ref[...], rows, 0, ext)
    for R in range(ext):
        for t in range(3):
            v = x[4 * R:4 * R + 4, t * LANES:(t + 1) * LANES]
            adj[R, t] = jnp.concatenate([v, v], axis=0)

    wait_rows(corners)

    def diffuse(g, c):
        for R in range(ext):
            for t in range(3):
                xi[g, R, t] = xi[g, R, t] * adj[R, t]
        for step in range(1, 2 * STEPS + 1):
            q = 0 if step <= STEPS else 2
            north = [xi[g, step - 1, t] for t in range(3)]
            center = [xi[g, step, t] for t in range(3)]
            for R in range(step, ext - step):
                south = [xi[g, R + 1, t] for t in range(3)]
                c0, c1, c2 = center
                sides = [pltpu.roll(c2, 1, 1) + c1, c0 + c2, c1 + pltpu.roll(c0, LANES - 1, 1)]
                for t in range(3):
                    xi[g, R, t] = (kk[q + 1, R, t] * center[t]
                                   + kk[q, R, t] * ((north[t] + south[t]) + sides[t]))
                north, center = center, south
        return c

    def chunk(c, carry):
        wait_rows(row_copies(c))
        lines = []
        for u in range(CHUNK):
            g = c * CHUNK + u
            lines += [one([nh[g, j, 0], nh[g, j, 1]], cn[g], 10 + j, cn[g], 2 + j) for j in range(HALO)]
            lines += [one([sh[g, j, 0], sh[g, j, 1]], cs[g], j, cs[g], 8 + j) for j in range(HALO)]
        x = moved(jnp.concatenate(lines, axis=0), into_ref[...], 2)
        for u in range(CHUNK):
            for j in range(2 * HALO):
                R = j if j < HALO else rows + j
                i = SUB * (u * 2 * HALO + j)
                for t in range(3):
                    xi[c * CHUNK + u, R, t] = x[i:i + SUB, t * LANES:(t + 1) * LANES]
        lax.fori_loop(c * CHUNK, (c + 1) * CHUNK, diffuse, 0)
        done(c).start()
        return carry

    def done(c):
        at = pl.ds(c * CHUNK, CHUNK)
        return pltpu.make_async_copy(xi.at[at, pl.ds(HALO, rows)], o_hbm.at[at], out_sem.at[c])

    lax.fori_loop(0, chunks, chunk, 0)
    for c in range(chunks):
        done(c).wait()
    every = got.at[pl.ds(1, n - 1), pl.ds(0, 5)]
    remote(every, every, send_sem, recv_sem.at[0], place(1)[1]).wait_send()


def whole(windows, k1, k2, view, mats, n_lat, n_lon):
    rows = k1.shape[0]
    ext = rows + 2 * HALO
    g = view.shape[0] // 512
    spec = pl.BlockSpec(memory_space=pltpu.VMEM)
    hbm = pl.BlockSpec(memory_space=pl.ANY)
    halo = [pltpu.VMEM((ext, 4, w * LANES), F32) for w in (2, 1, 1)]
    dma = pltpu.SemaphoreType.DMA
    return pl.pallas_call(
        lambda *refs: whole_kernel(n_lat, n_lon, *refs),
        out_shape=jax.ShapeDtypeStruct((g, rows, 3, SUB, LANES), F32),
        in_specs=[spec, spec, spec, hbm, spec, spec],
        out_specs=hbm,
        scratch_shapes=[
            pltpu.VMEM((rows, 4, 2 * LANES), F32),
            pltpu.VMEM(view.shape, F32),
            pltpu.VMEM((g, ext, 3, SUB, LANES), F32),
        ] + [pltpu.VMEM((g, HALO, 2, SUB, LANES), F32)] * 4
        + [pltpu.VMEM((g, 2, SUB, LANES), F32)] * 4
        + [pltpu.VMEM((g, SUB, LANES), F32)] * 4 + [
            pltpu.VMEM((4, ext, 3, SUB, LANES), F32),
            pltpu.VMEM((ext, 3, SUB, LANES), F32),
            pltpu.VMEM(windows.shape, F32),
            pltpu.VMEM((SUB * rows, 2 * LANES), F32),
            pltpu.VMEM((rows, 4, 2 * LANES), F32),
        ] + halo + halo + [dma, dma((8,))] + [dma((8,))] * 4
        + [dma((2, g // CHUNK))] * 2 + [dma((2,))] * 4 + [dma, dma((g // CHUNK,))],
        compiler_params=vmem(60, collective_id=0, has_side_effects=True),
        name="whole",
    )(windows, k1, k2, view, *mats)


def finish_kernel(x_ref, back_ref, o_ref):
    per, rows = x_ref.shape[:2]
    y = jnp.concatenate(
        [jnp.concatenate([x_ref[u, r, t] for t in range(3)], axis=1)
         for u in range(per) for r in range(rows)], axis=0)
    y = moved(y, back_ref[...], 2)
    for u in range(per):
        for r in range(rows):
            i = SUB * (u * rows + r)
            for ct in range(2):
                o_ref[pl.ds(512 * u + row_at(r, ct), SUB, stride=64), :] = (
                    y[i:i + SUB, ct * LANES:(ct + 1) * LANES])


def finish(x, back):
    g, rows = x.shape[:2]
    per = 2
    return pl.pallas_call(
        finish_kernel,
        grid=(g // per,),
        out_shape=jax.ShapeDtypeStruct((g * 512, LANES), F32),
        in_specs=[pl.BlockSpec((per,) + x.shape[1:], lambda i: (i, 0, 0, 0, 0)),
                  pl.BlockSpec(back.shape, lambda i: (0, 0))],
        out_specs=pl.BlockSpec((per * 512, LANES), lambda i: (i, 0)),
        compiler_params=vmem(40),
        name="finish",
    )(x, back)


def shards(innovation, jacobian, channel_count, owner, footprint, weight, perturbation,
           scale_first, scale_second):
    members, levels, rows, cols = perturbation.shape
    n_lat, n_lon = lax.axis_size("lat"), lax.axis_size("lon")
    fields = members * levels
    obs = innovation.shape[1]
    view = perturbation.reshape(fields, rows // SUB, SUB, cols // LANES, LANES)
    view = view.transpose(0, 1, 3, 2, 4).reshape(fields * 64, LANES)

    windows = pack(innovation, jacobian, channel_count.reshape(1, obs), owner.reshape(1, obs),
                   footprint, weight)
    *mats, back = layouts()
    out = whole(windows.reshape(n_lat * n_lon, 6, 4, LANES), scale_first, scale_second, view, mats,
                n_lat, n_lon)
    out = finish(out, back)
    out = out.reshape(fields, rows // SUB, cols // LANES, SUB, LANES).transpose(0, 1, 3, 2, 4)
    return out.reshape(members, levels, rows, cols)


def solution(mesh):
    both = ("lat", "lon")
    return jax.shard_map(
        shards,
        mesh=mesh,
        in_specs=(
            P(None, both),
            P(None, None, both),
            P(both),
            P(both, None),
            P(None, both),
            P(None, both),
            P(None, None, "lat", "lon"),
            P("lat", "lon"),
            P("lat", "lon"),
        ),
        out_specs=P(None, None, "lat", "lon"),
        check_vma=False,
    )
```

```python
import jax
import jax.numpy as jnp
import numpy as np
from jax import lax
from jax.experimental import pallas as pl
from jax.experimental.pallas import tpu as pltpu
from jax.sharding import PartitionSpec as P

STEPS = 3
HALO = 2 * STEPS
LANES = 128
SUB = 8
MESH = pl.DeviceIdType.MESH
F32 = jnp.float32
BF16 = jnp.bfloat16
I32 = jnp.int32
NT = (((1,), (1,)), ((), ()))


def iota(shape, dim):
    return lax.broadcasted_iota(I32, shape, dim)


def dot(a, b):
    return jnp.dot(a, b, preferred_element_type=F32)


def dot_nt(a, b):
    return lax.dot_general(a, b, NT, preferred_element_type=F32)


def vmem(limit, **kw):
    return pltpu.CompilerParams(vmem_limit_bytes=limit << 20, **kw)


def row_at(r, ct):
    return (r // SUB) * 16 + ct * SUB + r % SUB


def pack_kernel(inn_h, jac_h, cc_h, own_h, foot_h, wgt_h, out_ref,
                inn_ref, jac_ref, cc_ref, own_ref, foot_ref, wgt_ref,
                tot_ref, acc_ref, sorted_ref, cnt_v, cnt_s, sem, in_sem):
    chans, obs = inn_ref.shape
    blk = 256
    wide = 4 * blk
    loads = [pltpu.make_async_copy(h, v, in_sem.at[i]) for i, (h, v) in enumerate((
        (own_h, own_ref), (inn_h, inn_ref), (jac_h, jac_ref), (cc_h, cc_ref),
        (foot_h, foot_ref), (wgt_h, wgt_ref)))]
    for copy in loads:
        copy.start()
    loads[0].wait()
    hot_all = (iota((LANES, obs), 0) == own_ref[...]).astype(F32).astype(BF16)
    totals = dot(hot_all, jnp.ones((obs, LANES), BF16))
    tot_row = dot_nt(jnp.ones((SUB, obs), BF16), hot_all)
    upper = (iota((LANES, LANES), 0) < iota((LANES, LANES), 1)).astype(F32).astype(BF16)
    lower = (iota((LANES, LANES), 0) > iota((LANES, LANES), 1)).astype(F32).astype(BF16)
    cnt_v[0:SUB] = dot(tot_row.astype(BF16), upper).astype(I32)
    cnt_v[SUB:2 * SUB] = tot_row.astype(I32)
    to_smem = pltpu.make_async_copy(cnt_v, cnt_s, sem)
    to_smem.start()
    tot_ref[...] = dot(lower, totals.astype(BF16))
    upper_b = (iota((blk, blk), 0) < iota((blk, blk), 1)).astype(F32).astype(BF16)
    acc_ref[...] = jnp.zeros_like(acc_ref)
    for copy in loads[1:]:
        copy.wait()

    def block(i, carry):
        at = pl.ds(pl.multiple_of(i * wide, wide), wide)
        own = own_ref[:, at]
        hots = [iota((LANES, blk), 0) == own[:, j * blk:(j + 1) * blk] for j in range(4)]
        stack = jnp.concatenate([h.astype(F32).astype(BF16) for h in hots], axis=0)
        ranks = dot(stack, upper_b)
        sums = dot(stack, jnp.ones((blk, LANES), BF16))
        base = tot_ref[...]
        places = []
        for j in range(4):
            rank = ranks[LANES * j:LANES * (j + 1)] + jnp.concatenate([base, base], axis=1)
            places.append(jnp.sum(jnp.where(hots[j], rank, 0.0), axis=0, keepdims=True))
            base = base + sums[LANES * j:LANES * (j + 1)]
        tot_ref[...] = base
        pos = jnp.concatenate(places, axis=1).astype(I32)
        cc = cc_ref[:, at]
        prof = jnp.zeros((4, wide), F32)
        for c in range(chans):
            live = jnp.where(cc > c, inn_ref[c:c + 1, at], 0.0)
            prof = prof + jac_ref[c, :, at] * live
        full = jnp.concatenate([wgt_ref[:, at], foot_ref[:, at].astype(F32), prof, prof], axis=0)
        head = full.astype(BF16).astype(F32)
        both = jnp.concatenate([head, full - head], axis=0)
        hi = lax.shift_right_logical(pos, 8)
        lo = lax.bitwise_and(pos, 255)
        spread = jnp.concatenate(
            [jnp.where(hi == h, both, 0.0).astype(BF16) for h in range(obs // blk)], axis=0)
        hot_lo = (iota((blk, wide), 0) == lo).astype(F32).astype(BF16)
        acc_ref[...] += dot_nt(spread, hot_lo)
        return carry

    lax.fori_loop(0, obs // wide, block, 0)
    for h in range(obs // blk):
        s = acc_ref[48 * h:48 * h + 24, :] + acc_ref[48 * h + 24:48 * h + 48, :]
        sorted_ref[2 * h] = s[:, :LANES]
        sorted_ref[2 * h + 1] = s[:, LANES:]
    for t in range(2):
        sorted_ref[obs // LANES + t] = jnp.zeros((24, LANES), F32)
    to_smem.wait()
    lane = iota((24, LANES), 1)

    def window(i, carry):
        for u in range(4):
            d = i * 4 + u
            first = cnt_s[0, d]
            number = cnt_s[SUB, d]
            t = lax.shift_right_logical(first, 7)
            off = lax.bitwise_and(first, 127)
            y = jnp.where(lane >= off, sorted_ref[t], sorted_ref[t + 1])
            y = pltpu.roll(y, lax.bitwise_and(LANES - off, 127), 1)
            out_ref[pl.ds(pl.multiple_of(d * 24, 8), 24), :] = jnp.where(lane < number, y, 0.0)
        return carry

    lax.fori_loop(0, LANES // 4, window, 0)


def pack(inn, jac, cc, own, foot, wgt):
    obs = inn.shape[1]
    return pl.pallas_call(
        pack_kernel,
        out_shape=jax.ShapeDtypeStruct((24 * LANES, LANES), F32),
        in_specs=[pl.BlockSpec(memory_space=pl.ANY)] * 6,
        out_specs=pl.BlockSpec(memory_space=pltpu.VMEM),
        scratch_shapes=[pltpu.VMEM(a.shape, a.dtype) for a in (inn, jac, cc, own, foot, wgt)] + [
            pltpu.VMEM((LANES, LANES), F32),
            pltpu.VMEM((48 * (obs // 256), 256), F32),
            pltpu.VMEM((obs // LANES + 2, 24, LANES), F32),
            pltpu.VMEM((2 * SUB, LANES), I32),
            pltpu.SMEM((2 * SUB, LANES), I32),
            pltpu.SemaphoreType.DMA,
            pltpu.SemaphoreType.DMA((6,)),
        ],
        compiler_params=vmem(60),
        name="pack",
    )(inn, jac, cc, own, foot, wgt)


DIRS = ((1, 0), (-1, 0), (0, 1), (0, -1), (1, 1), (1, -1), (-1, 1), (-1, -1))


def halo_copies(src, mid, wb, eb, send, recv, n_lon):
    rows = src.shape[0]
    lat, lon = lax.axis_index("lat"), lax.axis_index("lon")
    copies = []
    for k, (dy, dx) in enumerate(DIRS):
        take = {1: pl.ds(rows - HALO, HALO), -1: pl.ds(0, HALO), 0: pl.ds(0, rows)}[dy]
        put = {1: pl.ds(0, HALO), -1: pl.ds(HALO + rows, HALO), 0: pl.ds(HALO, rows)}[dy]
        if dx == 0:
            s, d = src.at[take], mid.at[put]
        elif dx == 1:
            s, d = src.at[take, :, pl.ds(LANES, LANES)], wb.at[put]
        else:
            s, d = src.at[take, :, pl.ds(0, LANES)], eb.at[put]
        to = (lat + dy, lax.rem(lon + dx + n_lon, n_lon))
        copies.append(pltpu.make_async_remote_copy(
            src_ref=s, dst_ref=d, send_sem=send.at[k], recv_sem=recv.at[k],
            device_id=to, device_id_type=MESH))
    return copies


def when_lat(dy, lat, n_lat, fn):
    if dy == 0:
        fn()
    elif dy == 1:
        pl.when(lat < n_lat - 1)(fn)
    else:
        pl.when(lat > 0)(fn)


def halo_start(copies, lat, n_lat):
    for k, (dy, dx) in enumerate(DIRS):
        when_lat(dy, lat, n_lat, copies[k].start)


def halo_wait(copies, lat, n_lat):
    for k, (dy, dx) in enumerate(DIRS):
        when_lat(dy, lat, n_lat, copies[k].wait_send)
        when_lat(-dy, lat, n_lat, copies[k].wait_recv)


def halo_clear(mid, wb, eb, rows):
    for ref in (mid, wb, eb):
        for r in list(range(HALO)) + list(range(HALO + rows, 2 * HALO + rows)):
            ref[r] = jnp.zeros(ref.shape[1:], F32)


def lane_of(e):
    return (e % 3) * LANES + e // 3


def layouts():
    packed = np.zeros((4 * LANES, 3 * LANES), np.float32)
    whole = np.zeros((4 * LANES, 3 * LANES), np.float32)
    for c in range(2 * LANES):
        packed[c, lane_of(c + HALO)] = whole[c, lane_of(c + HALO)] = 1.0
    for q in range(LANES):
        if q % 8 >= 2:
            packed[2 * LANES + q, lane_of(q % 8 - 2)] = 1.0
        if q % 8 < HALO:
            packed[3 * LANES + q, lane_of(2 * LANES + HALO + q % 8)] = 1.0
    for q in range(HALO):
        whole[3 * LANES - HALO + q, lane_of(q)] = 1.0
        whole[3 * LANES + q, lane_of(2 * LANES + HALO + q)] = 1.0
    back = packed[:2 * LANES].T
    return [jnp.asarray(np.concatenate([m] * count), BF16)
            for m, count in ((whole, 3), (packed, 2), (back, 2))]


def moved(x, matrix, count):
    parts = []
    for _ in range(count - 1):
        head = x.astype(BF16)
        parts.append(head)
        x = x - head.astype(F32)
    return dot(jnp.concatenate(parts + [x.astype(BF16)], axis=1), matrix)


def interleaved(src, mid, wb, eb, whole, rows, start, count):
    lines = []
    for R in range(start, start + count):
        inner = src[R - HALO] if HALO <= R < HALO + rows else mid[R]
        lines.append(jnp.concatenate([inner, wb[R], eb[R]], axis=1))
    return moved(jnp.concatenate(lines, axis=0), whole, 3)


CHUNK = 4
BATCH = 8
MIX = 37


def whole_kernel(n_lat, n_lon, s_ref, k1_ref, k2_ref, p_hbm, whole_ref, into_ref, back_ref, o_hbm,
                 kap_ref, pv, xi, nsend, ssend, nh, sh, wsend, esend, pw, pe, tsend, bsend, cs, cn,
                 kk, adj, got, acc, sums, mid, wb, eb, mid2, wb2, eb2,
                 send_sem, recv_sem, hs, hr, hs2, hr2, row_s, row_r, col_s, col_r, cor_s, cor_r,
                 in_sem, out_sem):
    lat, lon = lax.axis_index("lat"), lax.axis_index("lon")
    n = n_lat * n_lon
    me = lat * n_lon + lon
    rows = kap_ref.shape[0]
    ext = rows + 2 * HALO
    fields8 = xi.shape[0]
    chunks = fields8 // CHUNK
    groups = recv_sem.shape[0]
    per = n // groups
    load = pltpu.make_async_copy(p_hbm, pv, in_sem)
    load.start()
    halo_clear(mid, wb, eb, rows)
    halo_clear(mid2, wb2, eb2, rows)
    bar = pltpu.get_barrier_semaphore()

    def place(k):
        t = lax.rem(me + k, n)
        return t, (lax.div(t, n_lon), lax.rem(t, n_lon))

    def signal(k, c):
        pl.semaphore_signal(bar, inc=1, device_id=place(k)[1], device_id_type=MESH)
        return c

    lax.fori_loop(1, n, signal, 0)
    for r in range(rows):
        k1, k2 = k1_ref[r:r + 1, :], k2_ref[r:r + 1, :]
        kap_ref[r] = jnp.concatenate([k1, 1.0 - 4.0 * k1, k2, 1.0 - 4.0 * k2], axis=0)

    @pl.when(lat == 0)
    def _():
        nh[...] = jnp.zeros_like(nh)
        cn[...] = jnp.zeros_like(cn)

    @pl.when(lat == n_lat - 1)
    def _():
        sh[...] = jnp.zeros_like(sh)
        cs[...] = jnp.zeros_like(cs)

    acc[...] = jnp.zeros_like(acc)
    pl.semaphore_wait(bar, n - 1)

    def send_group(g, first=0):
        def send(i, c):
            t, to = place(lax.rem(MIX * i, n))
            pltpu.make_async_remote_copy(
                src_ref=s_ref.at[t, pl.ds(0, 5)], dst_ref=got.at[i, pl.ds(0, 5)],
                send_sem=send_sem, recv_sem=recv_sem.at[g], device_id=to, device_id_type=MESH).start()
            return c

        lax.fori_loop(g * per + first, (g + 1) * per, send, 0)

    send_group(0, 1)
    send_group(1)
    kap_copies = halo_copies(kap_ref, mid, wb, eb, hs, hr, n_lon)
    halo_start(kap_copies, lat, n_lat)

    group = iota((SUB, LANES), 1) // SUB
    load.wait()

    def point(g, r, ct):
        return pv[pl.ds(512 * g + row_at(r, ct), SUB, stride=64), :]

    def edge(g, c):
        for r in range(HALO):
            for ct in range(2):
                nsend[g, r, ct] = point(g, r, ct)
                ssend[g, r, ct] = point(g, rows - HALO + r, ct)
        for b in range(2):
            w = jnp.zeros((SUB, LANES), F32)
            e = jnp.zeros((SUB, LANES), F32)
            for j in range(16):
                w = jnp.where(group == j, pltpu.roll(point(g, 16 * b + j, 0), 8 * j, 1), w)
                e = jnp.where(group == j, pltpu.roll(point(g, 16 * b + j, 1), (8 * j + 8) % LANES, 1), e)
            wsend[g, b] = w
            esend[g, b] = e
        return c

    lax.fori_loop(0, fields8, edge, 0)
    east, west = lax.rem(lon + 1, n_lon), lax.rem(lon + n_lon - 1, n_lon)

    def remote(src, dst, ss, rs, to):
        return pltpu.make_async_remote_copy(
            src_ref=src, dst_ref=dst, send_sem=ss, recv_sem=rs, device_id=to, device_id_type=MESH)

    cols = [remote(esend, pw, col_s.at[0], col_r.at[0], (lat, east)),
            remote(wsend, pe, col_s.at[1], col_r.at[1], (lat, west))]
    corners = [remote(bsend, cn, cor_s.at[0], cor_r.at[0], (lat + 1, lon)),
               remote(tsend, cs, cor_s.at[1], cor_r.at[1], (lat - 1, lon))]

    def row_copies(c):
        at = pl.ds(c * CHUNK, CHUNK)
        return [remote(ssend.at[at], nh.at[at], row_s.at[0, c], row_r.at[0, c], (lat + 1, lon)),
                remote(nsend.at[at], sh.at[at], row_s.at[1, c], row_r.at[1, c], (lat - 1, lon))]

    def start_rows(pair):
        pl.when(lat < n_lat - 1)(pair[0].start)
        pl.when(lat > 0)(pair[1].start)

    def wait_rows(pair):
        pl.when(lat < n_lat - 1)(pair[0].wait_send)
        pl.when(lat > 0)(pair[0].wait_recv)
        pl.when(lat > 0)(pair[1].wait_send)
        pl.when(lat < n_lat - 1)(pair[1].wait_recv)

    for copy in cols:
        copy.start()
    send_group(2)
    start_rows(row_copies(0))

    halo_wait(kap_copies, lat, n_lat)
    for half in range(2):
        x = interleaved(kap_ref, mid, wb, eb, whole_ref[...], rows, half * ext // 2, ext // 2)
        for i in range(ext // 2):
            for q in range(4):
                line = x[4 * i + q:4 * i + q + 1]
                for t in range(3):
                    kk[q, half * ext // 2 + i, t] = jnp.broadcast_to(
                        line[:, t * LANES:(t + 1) * LANES], (SUB, LANES))

    for copy in cols:
        copy.wait()

    def corner(g, c):
        tsend[g] = jnp.where(group < 6, pw[g, 0], pltpu.roll(pe[g, 0], 64, 1))
        bsend[g] = jnp.where(group >= 10, pw[g, 1], pltpu.roll(pe[g, 1], 64, 1))
        return c

    lax.fori_loop(0, fields8, corner, 0)
    start_rows(corners)

    def one(mid_rows, w, w_at, e, e_at):
        return jnp.concatenate(
            mid_rows + [jnp.where(group == w_at, w, 0.0), jnp.where(group == e_at, e, 0.0)], axis=1)

    def inner(c, carry):
        x = jnp.concatenate(
            [one([point(c * CHUNK + u, r, 0), point(c * CHUNK + u, r, 1)],
                 pw[c * CHUNK + u, r // 16], r % 16, pe[c * CHUNK + u, r // 16], r % 16)
             for u in range(CHUNK) for r in range(rows)], axis=0)
        x = moved(x, into_ref[...], 2)
        for u in range(CHUNK):
            for r in range(rows):
                i = SUB * (u * rows + r)
                for t in range(3):
                    xi[c * CHUNK + u, HALO + r, t] = x[i:i + SUB, t * LANES:(t + 1) * LANES]
        pl.when(c < 4)(lambda: send_group(3 + c))
        return carry

    lax.fori_loop(0, chunks, inner, 0)

    sub = iota((SUB, LANES), 0)
    row_ids = (iota((2 * LANES, LANES), 0) // SUB).astype(F32).astype(BF16)
    col_ids = iota((2 * LANES, LANES), 0).astype(F32).astype(BF16)

    def spread(block):
        w = jnp.concatenate([block[0], block[1]], axis=0)
        cell = jnp.concatenate([block[2], block[3]], axis=0).astype(I32)
        prof = jnp.concatenate([block[4], block[4]], axis=0)
        cell_row = lax.shift_right_logical(cell, 8).astype(F32).astype(BF16)
        cell_col = lax.bitwise_and(cell, 255).astype(F32).astype(BF16)
        left, right = [], []
        for f in range(SUB):
            v = w[f:f + 1] * prof
            head = v.astype(BF16).astype(F32)
            both = jnp.where(sub < 4, head, v - head).astype(BF16)
            both = jnp.concatenate([both] * 32, axis=0)
            left.append(jnp.where(row_ids == cell_row[f:f + 1], both, jnp.zeros_like(both)))
            right.append(jnp.where(col_ids == cell_col[f:f + 1], jnp.ones_like(both), jnp.zeros_like(both)))
        return left, right

    got[0] = s_ref[me]

    def add(i, c):
        left, right = [], []
        for u in range(BATCH):
            a, b = spread(got[i * BATCH + u])
            left += a
            right += b
        acc[...] += dot_nt(jnp.concatenate(left, axis=1), jnp.concatenate(right, axis=1))
        return c

    send_group(7)
    when_sent = {0: [1], 1: [2], 2: [3], 3: [4]}
    for g in range(groups):
        first, last = max(1, g * per), (g + 1) * per
        part = got.at[pl.ds(first, last - first), pl.ds(0, 5)]
        remote(part, part, send_sem, recv_sem.at[g], place(1)[1]).wait_recv()
        for c in when_sent.get(g, []):
            start_rows(row_copies(c))
        lax.fori_loop(g * per // BATCH, (g + 1) * per // BATCH, add, 0)

    for r in range(rows):
        x = acc[SUB * r:SUB * r + SUB, :]
        sums[r] = (x + pltpu.roll(x, 4, 0))[0:4]
    copies = halo_copies(sums, mid2, wb2, eb2, hs2, hr2, n_lon)
    halo_start(copies, lat, n_lat)
    halo_wait(copies, lat, n_lat)
    x = interleaved(sums, mid2, wb2, eb2, whole_ref[...], rows, 0, ext)
    for R in range(ext):
        for t in range(3):
            v = x[4 * R:4 * R + 4, t * LANES:(t + 1) * LANES]
            adj[R, t] = jnp.concatenate([v, v], axis=0)

    wait_rows(corners)

    def diffuse(g, c):
        for R in range(ext):
            for t in range(3):
                xi[g, R, t] = xi[g, R, t] * adj[R, t]
        for step in range(1, 2 * STEPS + 1):
            q = 0 if step <= STEPS else 2
            north = [xi[g, step - 1, t] for t in range(3)]
            center = [xi[g, step, t] for t in range(3)]
            for R in range(step, ext - step):
                south = [xi[g, R + 1, t] for t in range(3)]
                c0, c1, c2 = center
                sides = [pltpu.roll(c2, 1, 1) + c1, c0 + c2, c1 + pltpu.roll(c0, LANES - 1, 1)]
                for t in range(3):
                    xi[g, R, t] = (kk[q + 1, R, t] * center[t]
                                   + kk[q, R, t] * ((north[t] + south[t]) + sides[t]))
                north, center = center, south
        return c

    def chunk(c, carry):
        wait_rows(row_copies(c))
        lines = []
        for u in range(CHUNK):
            g = c * CHUNK + u
            lines += [one([nh[g, j, 0], nh[g, j, 1]], cn[g], 10 + j, cn[g], 2 + j) for j in range(HALO)]
            lines += [one([sh[g, j, 0], sh[g, j, 1]], cs[g], j, cs[g], 8 + j) for j in range(HALO)]
        x = moved(jnp.concatenate(lines, axis=0), into_ref[...], 2)
        for u in range(CHUNK):
            for j in range(2 * HALO):
                R = j if j < HALO else rows + j
                i = SUB * (u * 2 * HALO + j)
                for t in range(3):
                    xi[c * CHUNK + u, R, t] = x[i:i + SUB, t * LANES:(t + 1) * LANES]
        lax.fori_loop(c * CHUNK, (c + 1) * CHUNK, diffuse, 0)
        y = jnp.concatenate(
            [jnp.concatenate([xi[c * CHUNK + u, HALO + r, t] for t in range(3)], axis=1)
             for u in range(CHUNK) for r in range(rows)], axis=0)
        y = moved(y, back_ref[...], 2)
        for u in range(CHUNK):
            for r in range(rows):
                i = SUB * (u * rows + r)
                for ct in range(2):
                    pv[pl.ds(512 * (c * CHUNK + u) + row_at(r, ct), SUB, stride=64), :] = (
                        y[i:i + SUB, ct * LANES:(ct + 1) * LANES])
        done(c).start()
        return carry

    def done(c):
        at = pl.ds(c * CHUNK * 512, CHUNK * 512)
        return pltpu.make_async_copy(pv.at[at], o_hbm.at[at], out_sem.at[c])

    lax.fori_loop(0, chunks, chunk, 0)
    for c in range(chunks):
        done(c).wait()
    every = got.at[pl.ds(1, n - 1), pl.ds(0, 5)]
    remote(every, every, send_sem, recv_sem.at[0], place(1)[1]).wait_send()


def whole(windows, k1, k2, view, mats, n_lat, n_lon):
    rows = k1.shape[0]
    ext = rows + 2 * HALO
    g = view.shape[0] // 512
    spec = pl.BlockSpec(memory_space=pltpu.VMEM)
    hbm = pl.BlockSpec(memory_space=pl.ANY)
    halo = [pltpu.VMEM((ext, 4, w * LANES), F32) for w in (2, 1, 1)]
    dma = pltpu.SemaphoreType.DMA
    return pl.pallas_call(
        lambda *refs: whole_kernel(n_lat, n_lon, *refs),
        out_shape=jax.ShapeDtypeStruct(view.shape, F32),
        in_specs=[spec, spec, spec, hbm, spec, spec, spec],
        out_specs=hbm,
        scratch_shapes=[
            pltpu.VMEM((rows, 4, 2 * LANES), F32),
            pltpu.VMEM(view.shape, F32),
            pltpu.VMEM((g, ext, 3, SUB, LANES), F32),
        ] + [pltpu.VMEM((g, HALO, 2, SUB, LANES), F32)] * 4
        + [pltpu.VMEM((g, 2, SUB, LANES), F32)] * 4
        + [pltpu.VMEM((g, SUB, LANES), F32)] * 4 + [
            pltpu.VMEM((4, ext, 3, SUB, LANES), F32),
            pltpu.VMEM((ext, 3, SUB, LANES), F32),
            pltpu.VMEM(windows.shape, F32),
            pltpu.VMEM((SUB * rows, 2 * LANES), F32),
            pltpu.VMEM((rows, 4, 2 * LANES), F32),
        ] + halo + halo + [dma, dma((8,))] + [dma((8,))] * 4
        + [dma((2, g // CHUNK))] * 2 + [dma((2,))] * 4 + [dma, dma((g // CHUNK,))],
        compiler_params=vmem(60, collective_id=0, has_side_effects=True),
        name="whole",
    )(windows, k1, k2, view, *mats)


def place_kernel(x_ref, o_ref, buf, in_sem, out_sem):
    count = in_sem.shape[0]
    rows = x_ref.shape[0] // count
    parts = [pl.ds(i * rows, rows) for i in range(count)]
    loads = [pltpu.make_async_copy(x_ref.at[p], buf.at[p], in_sem.at[i]) for i, p in enumerate(parts)]
    stores = [pltpu.make_async_copy(buf.at[p], o_ref.at[p], out_sem.at[i]) for i, p in enumerate(parts)]
    for copy in loads:
        copy.start()
    for i in range(count):
        loads[i].wait()
        stores[i].start()
    for copy in stores:
        copy.wait()


def placed(x):
    hbm = pl.BlockSpec(memory_space=pl.ANY)
    return pl.pallas_call(
        place_kernel,
        out_shape=jax.ShapeDtypeStruct(x.shape, F32),
        in_specs=[hbm],
        out_specs=hbm,
        scratch_shapes=[pltpu.VMEM(x.shape, F32), pltpu.SemaphoreType.DMA((5,)),
                        pltpu.SemaphoreType.DMA((5,))],
        compiler_params=vmem(60),
        name="placed",
    )(x)


def shards(innovation, jacobian, channel_count, owner, footprint, weight, perturbation,
           scale_first, scale_second):
    members, levels, rows, cols = perturbation.shape
    n_lat, n_lon = lax.axis_size("lat"), lax.axis_size("lon")
    fields = members * levels
    obs = innovation.shape[1]
    view = perturbation.reshape(fields, rows // SUB, SUB, cols // LANES, LANES)
    view = view.transpose(0, 1, 3, 2, 4).reshape(fields * 64, LANES)

    windows = pack(innovation, jacobian, channel_count.reshape(1, obs), owner.reshape(1, obs),
                   footprint, weight)
    out = whole(windows.reshape(n_lat * n_lon, 6, 4, LANES), scale_first, scale_second, view, layouts(),
                n_lat, n_lon)
    out = placed(out)
    out = out.reshape(fields, rows // SUB, cols // LANES, SUB, LANES).transpose(0, 1, 3, 2, 4)
    return out.reshape(members, levels, rows, cols)


def solution(mesh):
    both = ("lat", "lon")
    return jax.shard_map(
        shards,
        mesh=mesh,
        in_specs=(
            P(None, both),
            P(None, None, both),
            P(both),
            P(both, None),
            P(None, both),
            P(None, both),
            P(None, None, "lat", "lon"),
            P("lat", "lon"),
            P("lat", "lon"),
        ),
        out_specs=P(None, None, "lat", "lon"),
        check_vma=False,
    )
```
